512 devices in a mesh: ctx: 64 (over y, z), kvh: 8 (over x, core).
Axes of the slice: x: 4, y: 8, z: 8, core: 2. Of those that a mesh axis runs over, the one named last changes fastest.
Arguments:
- queries: bfloat16 [256, 128, 128], P('ctx', 'kvh'), may hold values from -90 to 90
- cache_keys: bfloat16 [131072, 8, 128], P('ctx', 'kvh'), may hold values from -4 to 4
- cache_values: bfloat16 [131072, 8, 128], P('ctx', 'kvh'), may hold values from -6 to 6
- new_keys: bfloat16 [256, 8, 128], P('ctx', 'kvh'), may hold values from -4 to 4
- new_values: bfloat16 [256, 8, 128], P('ctx', 'kvh'), may hold values from -6 to 6
- cache_len: int32 [64], P('ctx'), may hold values from 1 to 2048, 81920 in all
- segment: int32 [256], replicated, may hold values from 0 to 3, never falling along the last dimension, each value on 1 to 128 neighbouring positions
- out_weight: bfloat16 [16384, 16384], P('kvh', 'ctx'), may hold values from -0.046875 to 0.046875
Outputs:
- mixed: bfloat16 [256, 16384], P('kvh', 'ctx')
The draws below stay inside these ranges and needn't reach their ends.
Inputs may be any that keep to these rules, and one draw needn't show every extreme that they name: `cache_len`: some shard holds 2048 live entries in every draw. `segment`: never falls along the tokens.
All inputs are finite; a program needn't handle non-finite values.
Results may differ from the reference program's by a relative error of at most 0.019.
Values may be sent and summed in bfloat16 or wider, within the bound.
No kernel may reach another device: no remote copies, remote signals or barrier semaphores. Data moves between devices by JAX's collectives and lax.ppermute only.
A program may use at most 64 MiB of HBM per device.

```python
import math
import jax
import jax.numpy as jnp
import numpy as np
from jax import lax

D = 16384
HEADS = 128
KVH = 8
HD = 128
CACHE_DEV = 2048
QB = 4
BRANCHES = 4
Q_TOK = 256
HIST = 81920
N_CTX = 64


def draw_queries(key, part):
    key = jax.random.fold_in(key, 11)
    base = jnp.clip(3.0 * jax.random.normal(key, (Q_TOK, HEADS, HD), jnp.float32), -18.0, 18.0)
    return base.astype(jnp.bfloat16)


def draw_cache_keys(key, part):
    key = jax.random.fold_in(key, 12)
    base = jnp.clip(jax.random.normal(key, (N_CTX * CACHE_DEV, KVH, HD), jnp.float32), -4.0, 4.0)
    return base.astype(jnp.bfloat16)


def levels(key, extent, cuts, least, high):
    level, own = 1.0, jax.random.fold_in(key, 6)
    for dim, parts in cuts:
        heights = jnp.exp(jax.random.uniform(jax.random.fold_in(own, dim), (parts,), jnp.float32, least / len(cuts), high / len(cuts)))
        level = level * jnp.repeat(heights, extent[dim] // parts).reshape([-1 if axis == dim else 1 for axis in range(len(extent))])
    return level


def length_profile(count, total, limit, slope):
    portions = [(1 << 20) // math.isqrt(standing ** slope) + 1 for standing in range(2, count + 1)]
    rest, holding = total - limit - (count - 1), [1] * (count - 1)
    while rest > 0:
        candidates = [i for i in range(count - 1) if holding[i] < limit]
        pool, remaining = sum([portions[i] for i in candidates]), rest
        for i in candidates:
            addition = min(limit - holding[i], max(1, remaining * portions[i] // pool), rest)
            holding[i] = holding[i] + addition
            rest = rest - addition
    return np.array([limit] + holding)


def uneven_parts(rng, count, total, bound, slope):
    if count == 2:
        one = jax.random.randint(rng, (), max(1, total - bound), min(bound, total - 1) + 1)
        return jnp.stack([one, total - one])
    lengths = jnp.asarray(length_profile(count, total, bound, slope), jnp.int32)
    pairs = (count - 1) // 2
    giver, receiver = lengths[1:1 + 2 * pairs:2], lengths[2:2 + 2 * pairs:2]
    room = jnp.minimum(giver - 1, bound - receiver)
    passed = jax.random.randint(jax.random.fold_in(rng, 1), (pairs,), 0, 1 << 20) % (room + 1)
    lengths = lengths.at[1:1 + 2 * pairs:2].set(giver - passed).at[2:2 + 2 * pairs:2].set(receiver + passed)
    return lengths[jax.random.permutation(jax.random.fold_in(rng, 2), count)]


def bell_draw(own_key, shape, scale, bound, pieces=(), kind=jnp.bfloat16):
    gain = levels(own_key, shape, pieces, -0.22, 0.18) if pieces else 1.0
    values = jax.random.normal(own_key, shape, jnp.float32) * scale * gain
    return jnp.minimum(jnp.maximum(values, -bound), bound).astype(kind)


def setup_inputs(seed: int = 0) -> dict:
    key_of = jax.random.split(jax.random.key(seed), 9)
    queries = draw_queries(jax.random.fold_in(key_of[8], 71), 0)
    cache_keys = draw_cache_keys(jax.random.fold_in(key_of[8], 71), 0)
    cache_values = bell_draw(key_of[2], (N_CTX * CACHE_DEV, KVH, HD), 1.0, 6.0, ((0, 64), (1, 8)))
    new_keys = bell_draw(key_of[3], (Q_TOK, KVH, HD), 1.0, 4.0, ((0, 64), (1, 8)))
    new_values = bell_draw(key_of[4], (Q_TOK, KVH, HD), 1.0, 6.0, ((0, 64), (1, 8)))
    cache_len = uneven_parts(key_of[5], N_CTX, HIST, CACHE_DEV, 2).astype(jnp.int32)
    segment = jnp.searchsorted(jnp.cumsum(uneven_parts(key_of[6], BRANCHES, Q_TOK, Q_TOK // 2, 1)), jnp.arange(Q_TOK), side="right").astype(jnp.int32)
    out_weight = bell_draw(key_of[7], (HEADS * HD, D), (HEADS * HD) ** -0.5, 0.046875, ((0, 8), (1, 64)))
    return dict(queries=queries, cache_keys=cache_keys, cache_values=cache_values, new_keys=new_keys, new_values=new_values, cache_len=cache_len, segment=segment, out_weight=out_weight)


def shard_part(rows, row_seg, row_pos, cache_k, cache_v, live, fresh_k, fresh_v, fresh_seg, fresh_pos):
    count_heads = rows.shape[1]
    group_size = count_heads // cache_k.shape[1]
    head_size = rows.shape[2]
    factor = 1.0 / (head_size ** 0.5)
    cache_ok = jnp.arange(cache_k.shape[0], dtype=jnp.int32) < live
    fresh_ok = (fresh_seg[None, :] == row_seg[:, None]) & (fresh_pos[None, :] <= row_pos[:, None])
    dims = (((1,), (1,)), ((), ()))

    def one_head(head):
        group = head // group_size
        query = lax.dynamic_index_in_dim(rows, head, 1, keepdims=False)
        keys_c = lax.dynamic_index_in_dim(cache_k, group, 1, keepdims=False)
        vals_c = lax.dynamic_index_in_dim(cache_v, group, 1, keepdims=False)
        keys_n = lax.dynamic_index_in_dim(fresh_k, group, 1, keepdims=False)
        vals_n = lax.dynamic_index_in_dim(fresh_v, group, 1, keepdims=False)
        score_c = lax.dot_general(query, keys_c, dims, preferred_element_type=jnp.float32) * factor
        score_n = lax.dot_general(query, keys_n, dims, preferred_element_type=jnp.float32) * factor
        score_c = jnp.where(cache_ok[None, :], score_c, -jnp.inf)
        score_n = jnp.where(fresh_ok, score_n, -jnp.inf)
        largest = jnp.maximum(jnp.max(score_c, axis=1), jnp.max(score_n, axis=1))
        weight_c = jnp.exp(score_c - largest[:, None]).astype(jnp.bfloat16)
        weight_n = jnp.exp(score_n - largest[:, None]).astype(jnp.bfloat16)
        totals = jnp.sum(weight_c.astype(jnp.float32), axis=1) + jnp.sum(weight_n.astype(jnp.float32), axis=1)
        result = jnp.dot(weight_c, vals_c, preferred_element_type=jnp.float32)
        result = result + jnp.dot(weight_n, vals_n, preferred_element_type=jnp.float32)
        return result, largest, totals

    outs, tops, totals = lax.map(one_head, jnp.arange(count_heads, dtype=jnp.int32))
    return jnp.transpose(outs, (1, 0, 2)), tops.T, totals.T


def reference(queries, cache_keys, cache_values, new_keys, new_values, cache_len, segment, out_weight):
    positions = jnp.arange(Q_TOK, dtype=jnp.int32)

    def fold(carry, shard):
        best, numer, denom = carry
        cache_k = lax.dynamic_slice_in_dim(cache_keys, shard * CACHE_DEV, CACHE_DEV, 0)
        cache_v = lax.dynamic_slice_in_dim(cache_values, shard * CACHE_DEV, CACHE_DEV, 0)
        fresh_k = lax.dynamic_slice_in_dim(new_keys, shard * QB, QB, 0)
        fresh_v = lax.dynamic_slice_in_dim(new_values, shard * QB, QB, 0)
        fresh_seg = lax.dynamic_slice_in_dim(segment, shard * QB, QB, 0)
        fresh_pos = shard * QB + jnp.arange(QB, dtype=jnp.int32)
        live = lax.dynamic_slice_in_dim(cache_len, shard, 1, 0)[0]
        outs, tops, totals = shard_part(queries, segment, positions, cache_k, cache_v, live,
                                        fresh_k, fresh_v, fresh_seg, fresh_pos)
        new_best = jnp.maximum(best, tops)
        old_scale = jnp.exp(best - new_best)
        this_scale = jnp.exp(tops - new_best)
        numer = numer * old_scale[..., None] + outs * this_scale[..., None]
        denom = denom * old_scale + totals * this_scale
        return (new_best, numer, denom), None

    start = (jnp.full((Q_TOK, HEADS), -jnp.inf, jnp.float32),
             jnp.zeros((Q_TOK, HEADS, HD), jnp.float32),
             jnp.zeros((Q_TOK, HEADS), jnp.float32))
    (best, numer, denom), unused = lax.scan(fold, start, jnp.arange(N_CTX, dtype=jnp.int32))
    attended = (numer / denom[..., None]).astype(jnp.bfloat16).reshape(Q_TOK, HEADS * HD)
    return jnp.dot(attended, out_weight, preferred_element_type=jnp.float32).astype(jnp.bfloat16)
```

```python
import functools

import jax
import jax.numpy as jnp
from jax import lax
from jax.experimental import pallas as pl
from jax.experimental.pallas import tpu as pltpu
from jax.sharding import PartitionSpec as P

BF = jnp.bfloat16
F32 = jnp.float32
LOG2E = 1.4426950408889634
LIMIT = 48 * 1024 * 1024
SIDE = 8
TAIL = 32
STEPS = ((0, 0), (0, 1), (1, 0), (-1, -1))


def shift(value, step):
    pairs = []
    for y in range(SIDE):
        for z in range(SIDE):
            to = ((y + step[0]) % SIDE) * SIDE + (z + step[1]) % SIDE
            pairs.append((y * SIDE + z, to))
    return lax.ppermute(value, "ctx", pairs)


def alike():
    half = range(SIDE // 2)
    return [
        [(2 * a + py) * SIDE + 2 * b + pz for a in half for b in half]
        for py in range(2)
        for pz in range(2)
    ]


def exchange(value):
    return lax.all_to_all(value, "ctx", 0, 0, axis_index_groups=alike(), tiled=True)


def quarters(value):
    copies = jnp.broadcast_to(value[None], (16,) + value.shape)
    mine = exchange(copies).reshape(16 * value.shape[0], value.shape[1])
    return [mine] + [shift(mine, step) for step in STEPS[1:]]


def call(body, out_shape, flops=0, moved=0, scratch=(), smem=0, args=()):
    vmem = pl.BlockSpec(memory_space=pltpu.VMEM)
    scalars = pl.BlockSpec(memory_space=pltpu.SMEM)
    specs = [scalars] * smem + [vmem] * (len(args) - smem)
    return pl.pallas_call(
        body,
        out_shape=out_shape,
        in_specs=specs,
        out_specs=jax.tree.map(lambda _: vmem, out_shape),
        scratch_shapes=list(scratch),
        compiler_params=pltpu.CompilerParams(vmem_limit_bytes=LIMIT),
        cost_estimate=pl.CostEstimate(flops=flops, bytes_accessed=moved, transcendentals=0),
    )(*args)


def prepare_body(live_ref, k_ref, v_ref, fk_ref, fv_ref, ka_ref, vt_ref):
    live = live_ref[0]
    slots, width = k_ref.shape
    step = 256
    first = k_ref[0:16, :].astype(F32)[0:1, :]
    for at in range(0, slots, step):
        alive = lax.broadcasted_iota(jnp.int32, (step, width), 0) + at < live
        keys = jnp.where(alive, k_ref[at : at + step, :].astype(F32), first)
        ka_ref[at : at + step, :] = keys.astype(BF)
        vals = jnp.where(alive, v_ref[at : at + step, :].astype(F32), 0.0)
        vt_ref[0:width, at : at + step] = vals.T.astype(BF)
        flags = lax.broadcasted_iota(jnp.int32, (16, step), 1) + at < live
        vt_ref[width:, at : at + step] = flags.astype(F32).astype(BF)
    ka_ref[slots:, :] = fk_ref[...]
    pad = jnp.zeros((128 - fv_ref.shape[0], width), F32)
    vt_ref[0:width, slots:] = jnp.concatenate([fv_ref[...].astype(F32), pad], 0).T.astype(BF)
    flags = lax.broadcasted_iota(jnp.int32, (16, 128), 1) < 4
    vt_ref[width:, slots:] = flags.astype(F32).astype(BF)


def prepare(live, keys, vals, fresh_k, fresh_v):
    slots, width = keys.shape
    out = [
        jax.ShapeDtypeStruct((slots + 16, width), BF),
        jax.ShapeDtypeStruct((width + 16, slots + 128), BF),
    ]
    return call(prepare_body, out, smem=1, args=(live, keys, vals, fresh_k, fresh_v))


def attend_body(step, place_ref, ka_ref, vt_ref, q_ref, o_ref, s0, s1, lse_ref):
    keys, width = ka_ref.shape
    slots = keys - 16
    rows = 256
    pieces = q_ref.shape[0] // rows
    factor = LOG2E / width**0.5
    y, z = place_ref[0], place_ref[1]
    first = 4 * (SIDE * y + z)
    from_y = lax.rem(y + SIDE - step[0], 2)
    from_z = lax.rem(z + SIDE - step[1], 2)
    lane = lax.broadcasted_iota(jnp.int32, (16, rows), 1)
    token0 = 8 * (lane // 64) + lax.rem(lane // 16, 4) + 32 * from_y + 4 * from_z
    line = lax.broadcasted_iota(jnp.int32, (16, rows), 0)
    never = 1 << 30
    opens = jnp.where(line < 4, line + first, never)
    ends = jnp.full((16, rows), never, jnp.int32)
    for j in range(4):
        ends = jnp.where(line == j, place_ref[4 + j], ends)
    scores = (s0, s1)
    cuts = [(at, 256) for at in range(0, slots, 256)] + [(slots, 16)]
    dims = (((1,), (1,)), ((), ()))

    def score(i, cut, best):
        at, deep = cut
        query = q_ref[i * rows : (i + 1) * rows, :]
        part = lax.dot_general(
            ka_ref[at : at + deep, :], query, dims, preferred_element_type=F32
        )
        if deep == 16:
            token = token0 + 64 * i
            part = jnp.where((token >= opens) & (token < ends), part, -jnp.inf)
        scores[i % 2][at : at + deep, :] = part
        top = jnp.max(part.reshape(deep // 8, 8, rows), axis=0)
        return top if best is None else jnp.maximum(best, top)

    def weigh(i, cut, peak, total):
        at, deep = cut
        part = scores[i % 2][at : at + deep, :]
        weight = jnp.exp2((part - peak) * factor).astype(BF)
        wide = deep
        if deep == 16:
            weight = jnp.concatenate([weight, jnp.zeros((112, rows), BF)], 0)
            wide = 128
        add = jnp.dot(vt_ref[:, at : at + wide], weight, preferred_element_type=F32)
        return add if total is None else total + add

    best = None
    for cut in cuts:
        best = score(0, cut, best)
    for i in range(pieces):
        peak = jnp.max(best, axis=0, keepdims=True)
        best, total = None, None
        for cut in cuts:
            if i + 1 < pieces:
                best = score(i + 1, cut, best)
            total = weigh(i, cut, peak, total)
        count = total[width : width + 1, :]
        out = total[0:width, :] * (1.0 / count)
        o_ref[i * rows : (i + 1) * rows, :] = out.T.astype(BF)
        lse = peak * factor + jnp.log(count) * LOG2E
        for b in range(rows // 128):
            at = i * (rows // 128) + b
            lse_ref[at : at + 1, :] = lse[:, b * 128 : (b + 1) * 128]
    o_ref[pieces * rows :, :] = parts_of(lse_ref[...], 8)


def parts_of(lse, lines):
    parts = []
    for _ in range(3):
        top = lse.astype(BF).astype(F32)
        parts.append(top)
        lse = lse - top
    parts.append(jnp.zeros((lines, 128), F32))
    return jnp.concatenate(parts, 0).astype(BF)


def attend(place, ka, vt, query, step):
    rows, width = query.shape
    keys = ka.shape[0]
    scratch = [pltpu.VMEM((keys, 256), F32)] * 2 + [pltpu.VMEM((8, 128), F32)]
    return call(
        functools.partial(attend_body, step),
        jax.ShapeDtypeStruct((rows + TAIL, width), BF),
        flops=8 * rows * keys * 256,
        moved=(ka.size + vt.size + 2 * query.size) * 2,
        scratch=scratch,
        smem=1,
        args=(place, ka, vt, query),
    )


def diagonal(rows):
    return lax.broadcasted_iota(jnp.int32, (rows, 128), 0) == lax.broadcasted_iota(
        jnp.int32, (rows, 128), 1
    )


def spread(row, eye):
    return jnp.sum(jnp.where(eye, row, 0.0), axis=1, keepdims=True)


def first_body(*refs):
    ins, out_ref = refs[:-1], refs[-1]
    rows = ins[0].shape[0] - TAIL
    eye = diagonal(128)
    logs = []
    for ref in ins:
        tail = ref[rows:, :].astype(F32)
        logs.append(tail[0:8] + tail[8:16] + tail[16:24])
    top = functools.reduce(jnp.maximum, logs)
    weights = [jnp.exp2(log - top) for log in logs]
    total = functools.reduce(jnp.add, weights)
    lse = top + jnp.log(total) * LOG2E
    weights = [w / total for w in weights]
    parts = []
    for _ in range(3):
        high = lse.astype(BF).astype(F32)
        parts.append(high)
        lse = lse - high
    empty = jnp.zeros((5, 128), F32)
    for b in range(rows // 128):
        merged = None
        for ref, weight in zip(ins, weights):
            term = ref[b * 128 : (b + 1) * 128, :].astype(F32) * spread(weight[b : b + 1], eye)
            merged = term if merged is None else merged + term
        merged = merged.astype(BF)
        tail = jnp.concatenate([p[b : b + 1] for p in parts] + [empty], 0).astype(BF)
        for j in range(2):
            out_ref[2 * b + j, 0:64, :] = merged[64 * j : 64 * j + 64, :]
            out_ref[2 * b + j, 64:72, :] = tail


def first_merge(ins):
    rows, width = ins[0].shape
    out = jax.ShapeDtypeStruct(((rows - TAIL) // 64, 72, width), BF)
    return call(first_body, out, args=tuple(ins))


def second_body(place_ref, got_ref, out_ref, logs):
    parts = got_ref.shape[0]
    for c in range(parts):
        tail = got_ref[c, 64:72, :].astype(F32)
        logs[c : c + 1, :] = tail[0:1] + tail[1:2] + tail[2:3]
    odd = lax.rem(place_ref[1] // 2, 2)
    lse = logs[...]
    lse = jnp.where(odd == 1, pltpu.roll(lse, 64, 1), lse)
    weight = jnp.exp2(lse - jnp.max(lse, axis=0, keepdims=True))
    weight = weight / jnp.sum(weight, axis=0, keepdims=True)
    eye = diagonal(64)
    total = None
    for c in range(parts):
        term = got_ref[c, 0:64, :].astype(F32) * spread(weight[c : c + 1, :], eye)
        total = term if total is None else total + term
    out_ref[...] = total.astype(BF)


def second_merge(place, got):
    return call(
        second_body,
        jax.ShapeDtypeStruct((64, got.shape[2]), BF),
        scratch=[pltpu.VMEM((got.shape[0], 128), F32)],
        smem=1,
        args=(place, got),
    )


def project_body(place_ref, w_ref, *refs):
    ins, out_ref, rows, left, placed = refs[:4], refs[4], refs[5], refs[6], refs[7]
    deep = w_ref.shape[0]
    width = ins[0].shape[1]
    heads = deep // width
    tokens = ins[0].shape[0] // heads
    for i, ref in enumerate(ins):
        rows[...] = ref[...].astype(F32)
        for h in range(heads):
            left[i * tokens : (i + 1) * tokens, h * width : (h + 1) * width] = rows[
                pl.ds(h, tokens, stride=heads), :
            ].astype(BF)
    mixed = jnp.dot(left[...], w_ref[...], preferred_element_type=F32)
    y, z = place_ref[0], place_ref[1]
    for i, step in enumerate(STEPS):
        from_y = lax.rem(y + SIDE - step[0], 2)
        from_z = lax.rem(z + SIDE - step[1], 2)
        for n in range(tokens // 4):
            to = 16 * (n // 4) + 2 * (n % 4) + 8 * from_y + from_z
            placed[to] = mixed[i * tokens + 4 * n : i * tokens + 4 * n + 4, :]
    for k in range(out_ref.shape[0]):
        out_ref[k] = jnp.concatenate([placed[8 * k + n] for n in range(8)], 0).astype(BF)


def project(place, weight, ins):
    deep, cols = weight.shape
    rows, width = ins[0].shape
    tokens = 4 * rows * width // deep
    return call(
        project_body,
        jax.ShapeDtypeStruct((8, tokens // 8, cols), BF),
        flops=2 * tokens * deep * cols,
        scratch=[
            pltpu.VMEM((rows, width), F32),
            pltpu.VMEM((tokens, deep), BF),
            pltpu.VMEM((tokens // 4, 4, cols), F32),
        ],
        smem=1,
        args=(place, weight, *ins),
    )


def final_body(got_ref, out_ref):
    total = got_ref[0].astype(F32)
    for i in range(1, got_ref.shape[0]):
        total = total + got_ref[i].astype(F32)
    out_ref[...] = total.astype(BF)


def local(queries, cache_keys, cache_values, new_keys, new_values, cache_len, segment, out_weight):
    me = lax.axis_index("ctx")
    block, heads, width = queries.shape
    asked = quarters(queries.reshape(block * heads, width))

    own_seg = lax.dynamic_slice_in_dim(segment, me * block, block, 0)
    ends = jnp.sum(segment[None, :] <= own_seg[:, None], axis=1).astype(jnp.int32)
    zero = jnp.zeros((), jnp.int32)
    place = jnp.concatenate([jnp.stack([me // SIDE, me % SIDE, zero, zero]), ends])

    pad = ((0, 16 - block), (0, 0))
    ka, vt = prepare(
        cache_len,
        cache_keys[:, 0, :],
        cache_values[:, 0, :],
        jnp.pad(new_keys[:, 0, :], pad),
        jnp.pad(new_values[:, 0, :], pad),
    )
    partial = [attend(place, ka, vt, q, step) for q, step in zip(asked, STEPS)]
    back = [shift(p, (-s[0], -s[1])) for p, s in zip(partial[1:], STEPS[1:])]
    own = second_merge(place, exchange(first_merge([partial[0]] + back)))
    parts = project(place, out_weight, quarters(own))
    got = lax.all_to_all(parts, "kvh", 0, 0, tiled=True)
    return call(final_body, jax.ShapeDtypeStruct(got.shape[1:], BF), args=(got,))


def solution(mesh):
    in_specs = (
        P("ctx", "kvh", None),
        P("ctx", "kvh", None),
        P("ctx", "kvh", None),
        P("ctx", "kvh", None),
        P("ctx", "kvh", None),
        P("ctx"),
        P(),
        P("kvh", "ctx"),
    )
    out_specs = P("kvh", "ctx")
    return jax.shard_map(local, mesh=mesh, in_specs=in_specs, out_specs=out_specs, check_vma=False)
```

```python
import jax
import jax.numpy as jnp
from jax import lax
from jax.experimental import pallas as pl
from jax.experimental.pallas import tpu as pltpu
from jax.sharding import PartitionSpec as P

BF = jnp.bfloat16
F32 = jnp.float32
LOG2E = 1.4426950408889634
LIMIT = 48 * 1024 * 1024
HUGE = 2.0**100


def call(body, out_shape, flops=0, moved=0, scratch=(), smem=0, args=()):
    vmem = pl.BlockSpec(memory_space=pltpu.VMEM)
    scalars = pl.BlockSpec(memory_space=pltpu.SMEM)
    specs = [scalars] * smem + [vmem] * (len(args) - smem)
    return pl.pallas_call(
        body,
        out_shape=out_shape,
        in_specs=specs,
        out_specs=jax.tree.map(lambda _: vmem, out_shape),
        scratch_shapes=list(scratch),
        compiler_params=pltpu.CompilerParams(vmem_limit_bytes=LIMIT),
        cost_estimate=pl.CostEstimate(flops=flops, bytes_accessed=moved, transcendentals=0),
    )(*args)


def copies(value, count):
    return jnp.broadcast_to(value[None], (count,) + value.shape)


def prepare_body(live_ref, k_ref, v_ref, fk_ref, fv_ref, ka_ref, vt_ref):
    live = live_ref[0]
    slots, width = k_ref.shape
    fresh = fk_ref.shape[0]
    step = 256
    first = k_ref[0:16, :].astype(F32)[0:1, :]
    for at in range(0, slots, step):
        alive = lax.broadcasted_iota(jnp.int32, (step, width), 0) + at < live
        keys = jnp.where(alive, k_ref[at : at + step, :].astype(F32), first)
        ka_ref[at : at + step, :] = keys.astype(BF)
        vals = jnp.where(alive, v_ref[at : at + step, :].astype(F32), 0.0)
        vt_ref[0:width, at : at + step] = vals.T.astype(BF)
        flags = lax.broadcasted_iota(jnp.int32, (16, step), 1) + at < live
        vt_ref[width:, at : at + step] = flags.astype(F32).astype(BF)
    keys = jnp.concatenate([fk_ref[...].astype(F32), jnp.zeros((16 - fresh, width), F32)], 0)
    ka_ref[slots:, :] = keys.astype(BF)
    vals = jnp.concatenate([fv_ref[...].astype(F32), jnp.zeros((128 - fresh, width), F32)], 0)
    vt_ref[0:width, slots:] = vals.T.astype(BF)
    flags = lax.broadcasted_iota(jnp.int32, (16, 128), 1) < fresh
    vt_ref[width:, slots:] = flags.astype(F32).astype(BF)


def prepare(live, keys, vals, fresh_k, fresh_v):
    slots, width = keys.shape
    out = [
        jax.ShapeDtypeStruct((slots + 16, width), BF),
        jax.ShapeDtypeStruct((width + 16, slots + 128), BF),
    ]
    return call(prepare_body, out, smem=1, args=(live, keys, vals, fresh_k, fresh_v))


def three(value):
    parts = []
    for _ in range(3):
        top = value.astype(BF).astype(F32)
        parts.append(top)
        value = value - top
    return parts


def attend_body(me_ref, seg_ref, ka_ref, vt_ref, q_ref, o_ref, worst_ref):
    keys, width = ka_ref.shape
    slots = keys - 16
    rows = 256
    heads = 16
    fresh = 4
    pieces = q_ref.shape[0] // rows
    factor = LOG2E / width**0.5
    first = fresh * me_ref[0]
    line = lax.broadcasted_iota(jnp.int32, (16, rows), 0)
    never = 1 << 30
    opens = jnp.where(line < fresh, line + first, never)
    ends = jnp.full((16, rows), never, jnp.int32)
    seg = seg_ref[...]
    spot = lax.broadcasted_iota(jnp.int32, seg.shape, 0) * 128 + lax.broadcasted_iota(
        jnp.int32, seg.shape, 1
    )
    for j in range(fresh):
        own = jnp.sum(jnp.where(spot == first + j, seg, 0))
        ends = jnp.where(line == j, jnp.sum((seg <= own).astype(jnp.int32)), ends)
    token0 = lax.broadcasted_iota(jnp.int32, (16, rows), 1) // heads
    cuts = [(at, 256) for at in range(0, slots, 256)] + [(slots, 16)]

    def score(query, cut, i):
        at, deep = cut
        part = jnp.dot(ka_ref[at : at + deep, :], query, preferred_element_type=F32)
        if deep == 16:
            token = token0 + i * (rows // heads)
            part = jnp.where((token >= opens) & (token < ends), part, -jnp.inf)
        return part

    def most(part):
        return jnp.max(part, axis=0, keepdims=True)

    def piece(i, exact):
        at = pl.multiple_of(i * rows, rows)
        query = q_ref[pl.ds(at, rows), :].astype(F32).T.astype(BF)
        start = score(query, cuts[0], i)
        peak = most(start)
        if exact:
            for cut in cuts[1:]:
                peak = jnp.maximum(peak, most(score(query, cut, i)))
        total = None
        for n, cut in enumerate(cuts):
            part = start if n == 0 else score(query, cut, i)
            weight = jnp.exp2((part - peak) * factor).astype(BF)
            wide = cut[1]
            if wide == 16:
                weight = jnp.concatenate([weight, jnp.zeros((112, rows), BF)], 0)
                wide = 128
            add = jnp.dot(vt_ref[:, cut[0] : cut[0] + wide], weight, preferred_element_type=F32)
            total = add if total is None else total + add
        count = total[width : width + 1, :]
        out = (total[0:width, :] * (1.0 / count)).T.astype(BF)
        parts = three(peak * factor + jnp.log(count) * LOG2E)
        empty = jnp.zeros((5, 128), F32)
        for j in range(rows // 64):
            to = i * (rows // 64) + j
            lanes = slice(128 * (j // 2), 128 * (j // 2) + 128)
            o_ref[to, 0:64, :] = out[64 * j : 64 * j + 64, :]
            tail = jnp.concatenate([p[:, lanes] for p in parts] + [empty], 0)
            o_ref[to, 64:72, :] = tail.astype(BF)
        return count

    worst_ref[...] = jnp.zeros(worst_ref.shape, F32)

    def quick(i, carry):
        counts = jnp.maximum(piece(2 * i, False), piece(2 * i + 1, False))
        worst_ref[0:1, :] = jnp.maximum(worst_ref[0:1, :], counts)
        return carry

    lax.fori_loop(0, pieces // 2, quick, 0)

    @pl.when(jnp.logical_not(jnp.max(worst_ref[0:1, :]) < HUGE))
    def _():
        def slow(i, carry):
            piece(i, True)
            return carry

        lax.fori_loop(0, pieces, slow, 0)


def attend(me, seg, ka, vt, query):
    rows, width = query.shape
    return call(
        attend_body,
        jax.ShapeDtypeStruct((rows // 64, 72, width), BF),
        flops=8 * rows * ka.shape[0] * 256,
        moved=(ka.size + vt.size + 2 * query.size) * 2,
        scratch=[pltpu.VMEM((8, 256), F32)],
        smem=1,
        args=(me, seg, ka, vt, query),
    )


def merge_body(me_ref, got_ref, out_ref, logs):
    parts = got_ref.shape[0]
    for c in range(parts):
        tail = got_ref[c, 64:72, :].astype(F32)
        logs[c : c + 1, :] = tail[0:1] + tail[1:2] + tail[2:3]
    lse = logs[...]
    lse = jnp.where(lax.rem(me_ref[0], 2) == 1, pltpu.roll(lse, 64, 1), lse)
    weight = jnp.exp2(lse - jnp.max(lse, axis=0, keepdims=True))
    weight = weight / jnp.sum(weight, axis=0, keepdims=True)
    eye = lax.broadcasted_iota(jnp.int32, (64, 128), 0) == lax.broadcasted_iota(
        jnp.int32, (64, 128), 1
    )
    total = None
    for c in range(parts):
        column = jnp.sum(jnp.where(eye, weight[c : c + 1, :], 0.0), axis=1, keepdims=True)
        term = got_ref[c, 0:64, :].astype(F32) * column
        total = term if total is None else total + term
    out_ref[...] = total.astype(BF)


def merge(me, got):
    return call(
        merge_body,
        jax.ShapeDtypeStruct((64, got.shape[2]), BF),
        scratch=[pltpu.VMEM((got.shape[0], 128), F32)],
        smem=1,
        args=(me, got),
    )


def project_body(w_ref, in_ref, out_ref, rows):
    heads = w_ref.shape[0] // in_ref.shape[1]
    tokens = in_ref.shape[0] // heads
    rows[...] = in_ref[...].astype(F32)
    left = [rows[pl.ds(h, tokens, stride=heads), :].astype(BF) for h in range(heads)]
    mixed = jnp.dot(jnp.concatenate(left, 1), w_ref[...], preferred_element_type=F32)
    out_ref[...] = mixed.astype(BF)


def project(weight, value):
    deep, cols = weight.shape
    tokens = value.size // deep
    return call(
        project_body,
        jax.ShapeDtypeStruct((tokens, cols), BF),
        flops=2 * tokens * deep * cols,
        scratch=[pltpu.VMEM(value.shape, F32)],
        args=(weight, value),
    )


def final_body(got_ref, out_ref):
    total = got_ref[0].astype(F32)
    for i in range(1, got_ref.shape[0]):
        total = total + got_ref[i].astype(F32)
    out_ref[...] = total.astype(BF)


def local(queries, cache_keys, cache_values, new_keys, new_values, cache_len, segment, out_weight):
    me = lax.axis_index("ctx").reshape(1).astype(jnp.int32)
    ring = lax.axis_size("ctx")
    block, heads, width = queries.shape
    own = copies(queries.reshape(block * heads, width), ring)
    asked = lax.all_to_all(own, "ctx", 0, 0, tiled=True).reshape(-1, width)
    ka, vt = prepare(
        cache_len,
        cache_keys[:, 0, :],
        cache_values[:, 0, :],
        new_keys[:, 0, :],
        new_values[:, 0, :],
    )
    partial = attend(me, segment.reshape(-1, 128), ka, vt, asked)
    own = merge(me, lax.all_to_all(partial, "ctx", 0, 0, tiled=True))
    every = lax.all_to_all(copies(own, ring), "ctx", 0, 0, tiled=True).reshape(-1, width)
    mixed = project(out_weight, every)
    mixed = mixed.reshape(lax.axis_size("kvh"), -1, mixed.shape[1])
    got = lax.all_to_all(mixed, "kvh", 0, 0, tiled=True)
    return call(final_body, jax.ShapeDtypeStruct(got.shape[1:], BF), args=(got,))


def solution(mesh):
    in_specs = (
        P("ctx", "kvh", None),
        P("ctx", "kvh", None),
        P("ctx", "kvh", None),
        P("ctx", "kvh", None),
        P("ctx", "kvh", None),
        P("ctx"),
        P(),
        P("kvh", "ctx"),
    )
    out_specs = P("kvh", "ctx")
    return jax.shard_map(local, mesh=mesh, in_specs=in_specs, out_specs=out_specs, check_vma=False)
```

```python
import jax
import jax.numpy as jnp
from jax import lax
from jax.experimental import pallas as pl
from jax.experimental.pallas import tpu as pltpu
from jax.sharding import PartitionSpec as P

BF = jnp.bfloat16
F32 = jnp.float32
LOG2E = 1.4426950408889634
LIMIT = 48 * 1024 * 1024
HUGE = 2.0**100
SIDE = 8
STEPS = ((0, 0), (1, 0), (-1, 0), (0, 1))
BLOCK = 512


def shift(value, step):
    pairs = []
    for y in range(SIDE):
        for z in range(SIDE):
            to = ((y + step[0]) % SIDE) * SIDE + (z + step[1]) % SIDE
            pairs.append((y * SIDE + z, to))
    return lax.ppermute(value, "ctx", pairs)


def coset(y, z):
    return lax.rem(y + 2 * z + 4 * SIDE, 4)


def member_y(which, i):
    return lax.rem(which + 2 * (i // 2), 4) + 4 * (i % 2)


def cosets():
    return [
        [((v + 2 * z) % 4 + 4 * b) * SIDE + z for z in range(SIDE) for b in range(2)]
        for v in range(4)
    ]


def exchange(value):
    return lax.all_to_all(value, "ctx", 0, 0, axis_index_groups=cosets(), tiled=True)


def share(value):
    copies = jnp.broadcast_to(value[None], (16,) + value.shape)
    return exchange(copies).reshape(16 * value.shape[0], value.shape[1])


def call(body, out_shape, flops=0, moved=0, scratch=(), smem=0, args=()):
    vmem = pl.BlockSpec(memory_space=pltpu.VMEM)
    scalars = pl.BlockSpec(memory_space=pltpu.SMEM)
    specs = [scalars] * smem + [vmem] * (len(args) - smem)
    return pl.pallas_call(
        body,
        out_shape=out_shape,
        in_specs=specs,
        out_specs=jax.tree.map(lambda _: vmem, out_shape),
        scratch_shapes=list(scratch),
        compiler_params=pltpu.CompilerParams(vmem_limit_bytes=LIMIT),
        cost_estimate=pl.CostEstimate(flops=flops, bytes_accessed=moved, transcendentals=0),
    )(*args)


def pack_body(live_ref, k_ref, v_ref, fk_ref, fv_ref, out_ref):
    live = live_ref[0]
    slots, width = k_ref.shape
    fresh = fk_ref.shape[0]
    span = slots + 16
    step = 256
    first = k_ref[0:16, :].astype(F32)[0:1, :]
    for at in range(0, slots, step):
        alive = lax.broadcasted_iota(jnp.int32, (step, width), 0) + at < live
        keys = jnp.where(alive, k_ref[at : at + step, :].astype(F32), first)
        out_ref[at : at + step, :] = keys.astype(BF)
        vals = jnp.where(alive, v_ref[at : at + step, :].astype(F32), 0.0)
        out_ref[span + at : span + at + step, :] = vals.astype(BF)
    pad = jnp.zeros((16 - fresh, width), F32)
    for at, ref in ((slots, fk_ref), (span + slots, fv_ref)):
        out_ref[at : at + 16, :] = jnp.concatenate([ref[...].astype(F32), pad], 0).astype(BF)
    line = lax.broadcasted_iota(jnp.int32, (16, width), 0)
    size = jnp.where(line == 0, live // 64, jnp.where(line == 1, lax.rem(live, 64), 0))
    out_ref[2 * span :, :] = size.astype(F32).astype(BF)


def pack(live, keys, vals, fresh_k, fresh_v):
    slots, width = keys.shape
    out = jax.ShapeDtypeStruct((2 * (slots + 16) + 16, width), BF)
    return call(pack_body, out, smem=1, args=(live, keys, vals, fresh_k, fresh_v))


def three(value):
    parts = []
    for _ in range(3):
        top = value.astype(BF).astype(F32)
        parts.append(top)
        value = value - top
    return parts


def attend_body(place_ref, seg_ref, q_ref, *refs):
    shards, (o_ref, peak_ref, sum_ref) = refs[:4], refs[4:]
    rows, width = q_ref.shape
    span = (shards[0].shape[0] - 16) // 2
    slots = span - 16
    heads = 16
    fresh = 4
    factor = LOG2E / width**0.5
    y, z = place_ref[0], place_ref[1]
    dims = (((1,), (1,)), ((), ()))
    lives = []
    for ref in shards:
        size = ref[2 * span :, :].astype(F32)
        lives.append(jnp.max(64.0 * size[0:1] + size[1:2]).astype(jnp.int32))

    def score(keys):
        return lax.dot_general(q_ref[...], keys, dims, preferred_element_type=F32)

    def weigh(part):
        peak = peak_ref[...]
        lanes = [part[:, at : at + 128] - peak for at in range(0, part.shape[1], 128)]
        lanes = [jnp.exp2(lane * factor).astype(BF) for lane in lanes]
        return jnp.concatenate(lanes, 1) if len(lanes) > 1 else lanes[0]

    def beside(vals, ones):
        return jnp.concatenate([vals, ones.astype(F32).astype(BF)], 1)

    def most(part):
        return jnp.broadcast_to(jnp.max(part, axis=1, keepdims=True), (rows, 128))

    seg = seg_ref[...]
    spot = lax.broadcasted_iota(jnp.int32, seg.shape, 0) * 128 + lax.broadcasted_iota(
        jnp.int32, seg.shape, 1
    )
    lane = lax.broadcasted_iota(jnp.int32, (8, 128), 1)
    never = 1 << 30
    opens = jnp.full((8, 128), never, jnp.int32)
    ends = jnp.full((8, 128), never, jnp.int32)
    for s, step in enumerate(STEPS):
        from_y = lax.rem(y + SIDE - step[0], SIDE)
        from_z = lax.rem(z + SIDE - step[1], SIDE)
        for j in range(fresh):
            token = fresh * (SIDE * from_y + from_z) + j
            own = jnp.sum(jnp.where(spot == token, seg, 0))
            here = lane == 16 * s + j
            opens = jnp.where(here, token, opens)
            ends = jnp.where(here, jnp.sum((seg <= own).astype(jnp.int32)), ends)
    opens, ends = opens[0:1], ends[0:1]

    def fresh_score():
        pad = jnp.zeros((64, width), BF)
        part = score(jnp.concatenate([r[slots:span, :] for r in shards] + [pad], 0))
        line = lax.broadcasted_iota(jnp.int32, (rows, 128), 0)
        member = line // 64
        token = 32 * member_y(coset(y, z), member) + 4 * (member // 2)
        token = token + lax.rem(line // heads, 4)
        return jnp.where((token >= opens) & (token < ends), part, -jnp.inf)

    def gather():
        pad = jnp.zeros((64, width), BF)
        vals = jnp.concatenate([r[span + slots : 2 * span, :] for r in shards] + [pad], 0)
        ones = lax.broadcasted_iota(jnp.int32, (128, 128), 0)
        ones = (lax.rem(ones, 16) < fresh) & (ones < 64)
        sum_ref[...] = jnp.dot(
            weigh(fresh_score()), beside(vals, ones), preferred_element_type=F32
        )
        for ref, live in zip(shards, lives):

            def step(n, carry, ref=ref, live=live):
                at = pl.multiple_of(n * BLOCK, BLOCK)
                keys = ref[pl.ds(at, BLOCK), :]
                vals = ref[pl.ds(pl.multiple_of(span + at, 16), BLOCK), :]
                ones = lax.broadcasted_iota(jnp.int32, (BLOCK, 128), 0) + at < live
                sum_ref[...] += jnp.dot(
                    weigh(score(keys)), beside(vals, ones), preferred_element_type=F32
                )
                return carry

            lax.fori_loop(0, (live + BLOCK - 1) // BLOCK, step, 0)

    peak_ref[...] = most(score(shards[0][0:256, :]))
    gather()

    @pl.when(jnp.logical_not(jnp.max(sum_ref[:, width:]) < HUGE))
    def _():
        peak_ref[...] = jnp.maximum(peak_ref[...], most(fresh_score()))
        for ref, live in zip(shards, lives):

            def step(n, carry, ref=ref):
                at = pl.multiple_of(n * BLOCK, BLOCK)
                part = score(ref[pl.ds(at, BLOCK), :])
                peak_ref[...] = jnp.maximum(peak_ref[...], most(part))
                return carry

            lax.fori_loop(0, (live + BLOCK - 1) // BLOCK, step, 0)
        gather()

    eye = lax.broadcasted_iota(jnp.int32, (128, 128), 0) == lax.broadcasted_iota(
        jnp.int32, (128, 128), 1
    )
    empty = jnp.zeros((5, 128), F32)
    for b in range(rows // 128):
        at = slice(128 * b, 128 * b + 128)
        count = sum_ref[at, width:]
        out = (sum_ref[at, 0:width] / count).astype(BF)
        lse = peak_ref[at, :] * factor + jnp.log(count) * LOG2E
        row = jnp.sum(jnp.where(eye, lse, 0.0), axis=0, keepdims=True)
        tail = jnp.concatenate(three(row) + [empty], 0).astype(BF)
        for j in range(2):
            o_ref[2 * b + j, 0:64, :] = out[64 * j : 64 * j + 64, :]
            o_ref[2 * b + j, 64:72, :] = tail


def attend(place, seg, query, shards):
    rows, width = query.shape
    keys = 4 * shards[0].shape[0] // 2
    return call(
        attend_body,
        jax.ShapeDtypeStruct((rows // 64, 72, width), BF),
        flops=8 * rows * keys * 256,
        moved=(4 * shards[0].size + 2 * query.size) * 2,
        scratch=[pltpu.VMEM((rows, 128), F32), pltpu.VMEM((rows, 2 * width), F32)],
        smem=1,
        args=(place, seg, query, *shards),
    )


def merge_body(place_ref, got_ref, out_ref, logs):
    parts = got_ref.shape[0]
    for c in range(parts):
        tail = got_ref[c, 64:72, :].astype(F32)
        logs[c : c + 1, :] = tail[0:1] + tail[1:2] + tail[2:3]
    lse = logs[...]
    lse = jnp.where(place_ref[0] // 4 == 1, pltpu.roll(lse, 64, 1), lse)
    weight = jnp.exp2(lse - jnp.max(lse, axis=0, keepdims=True))
    weight = weight / jnp.sum(weight, axis=0, keepdims=True)
    eye = lax.broadcasted_iota(jnp.int32, (64, 128), 0) == lax.broadcasted_iota(
        jnp.int32, (64, 128), 1
    )
    total = None
    for c in range(parts):
        column = jnp.sum(jnp.where(eye, weight[c : c + 1, :], 0.0), axis=1, keepdims=True)
        term = got_ref[c, 0:64, :].astype(F32) * column
        total = term if total is None else total + term
    out_ref[...] = total.astype(BF)


def merge(place, got):
    return call(
        merge_body,
        jax.ShapeDtypeStruct((64, got.shape[2]), BF),
        scratch=[pltpu.VMEM((got.shape[0], 128), F32)],
        smem=1,
        args=(place, got),
    )


def project_body(place_ref, w_ref, *refs):
    ins, out_ref, rows, placed = refs[:4], refs[4], refs[5], refs[6]
    heads = w_ref.shape[0] // ins[0].shape[1]
    tokens = ins[0].shape[0] // heads
    left = []
    for ref in ins:
        rows[...] = ref[...].astype(F32)
        parts = [rows[pl.ds(h, tokens, stride=heads), :].astype(BF) for h in range(heads)]
        left.append(jnp.concatenate(parts, 1))
    mixed = jnp.dot(jnp.concatenate(left, 0), w_ref[...], preferred_element_type=F32)
    for i, step in enumerate(STEPS):
        which = coset(place_ref[0] - step[0], place_ref[1] - step[1])
        for n in range(tokens // 4):
            to = SIDE * member_y(which, n) + n // 2
            placed[to] = mixed[i * tokens + 4 * n : i * tokens + 4 * n + 4, :]
    for k in range(out_ref.shape[0]):
        out_ref[k] = jnp.concatenate([placed[8 * k + n] for n in range(8)], 0).astype(BF)


def project(place, weight, ins):
    deep, cols = weight.shape
    rows, width = ins[0].shape
    tokens = 4 * rows * width // deep
    return call(
        project_body,
        jax.ShapeDtypeStruct((8, tokens // 8, cols), BF),
        flops=2 * tokens * deep * cols,
        scratch=[pltpu.VMEM((rows, width), F32), pltpu.VMEM((tokens // 4, 4, cols), F32)],
        smem=1,
        args=(place, weight, *ins),
    )


def final_body(got_ref, out_ref):
    total = got_ref[0].astype(F32)
    for i in range(1, got_ref.shape[0]):
        total = total + got_ref[i].astype(F32)
    out_ref[...] = total.astype(BF)


def local(queries, cache_keys, cache_values, new_keys, new_values, cache_len, segment, out_weight):
    me = lax.axis_index("ctx").astype(jnp.int32)
    place = jnp.stack([me // SIDE, me % SIDE])
    block, heads, width = queries.shape
    shard = pack(
        cache_len,
        cache_keys[:, 0, :],
        cache_values[:, 0, :],
        new_keys[:, 0, :],
        new_values[:, 0, :],
    )
    shards = [shard] + [shift(shard, step) for step in STEPS[1:]]
    asked = share(queries.reshape(block * heads, width))
    partial = attend(place, segment.reshape(-1, 128), asked, shards)
    own = merge(place, exchange(partial))
    mine = share(own)
    every = [mine] + [shift(mine, step) for step in STEPS[1:]]
    mixed = project(place, out_weight, every)
    got = lax.all_to_all(mixed, "kvh", 0, 0, tiled=True)
    return call(final_body, jax.ShapeDtypeStruct(got.shape[1:], BF), args=(got,))


def solution(mesh):
    in_specs = (
        P("ctx", "kvh", None),
        P("ctx", "kvh", None),
        P("ctx", "kvh", None),
        P("ctx", "kvh", None),
        P("ctx", "kvh", None),
        P("ctx"),
        P(),
        P("kvh", "ctx"),
    )
    out_specs = P("kvh", "ctx")
    return jax.shard_map(local, mesh=mesh, in_specs=in_specs, out_specs=out_specs, check_vma=False)
```

```python
import functools

import jax
import jax.numpy as jnp
from jax import lax
from jax.experimental import pallas as pl
from jax.experimental.pallas import tpu as pltpu
from jax.sharding import PartitionSpec as P

BF = jnp.bfloat16
F32 = jnp.float32
LOG2E = 1.4426950408889634
LIMIT = 48 * 1024 * 1024
HUGE = 2.0**100
SIDE = 8
STEPS = ((0, 0), (1, 0), (-1, 0), (0, 1))
TAIL = 32


def shift(value, step):
    pairs = []
    for y in range(SIDE):
        for z in range(SIDE):
            to = ((y + step[0]) % SIDE) * SIDE + (z + step[1]) % SIDE
            pairs.append((y * SIDE + z, to))
    return lax.ppermute(value, "ctx", pairs)


def coset(y, z):
    return lax.rem(y + 2 * z + 4 * SIDE, 4)


def member_y(which, i):
    return lax.rem(which + 2 * (i // 2), 4) + 4 * (i % 2)


def cosets():
    return [
        [((v + 2 * z) % 4 + 4 * b) * SIDE + z for z in range(SIDE) for b in range(2)]
        for v in range(4)
    ]


def exchange(value):
    return lax.all_to_all(value, "ctx", 0, 0, axis_index_groups=cosets(), tiled=True)


def share(value):
    copies = jnp.broadcast_to(value[None], (16,) + value.shape)
    return exchange(copies).reshape(16 * value.shape[0], value.shape[1])


def call(body, out_shape, flops=0, moved=0, scratch=(), smem=0, args=()):
    vmem = pl.BlockSpec(memory_space=pltpu.VMEM)
    scalars = pl.BlockSpec(memory_space=pltpu.SMEM)
    specs = [scalars] * smem + [vmem] * (len(args) - smem)
    return pl.pallas_call(
        body,
        out_shape=out_shape,
        in_specs=specs,
        out_specs=jax.tree.map(lambda _: vmem, out_shape),
        scratch_shapes=list(scratch),
        compiler_params=pltpu.CompilerParams(vmem_limit_bytes=LIMIT),
        cost_estimate=pl.CostEstimate(flops=flops, bytes_accessed=moved, transcendentals=0),
    )(*args)


def prepare_body(live_ref, k_ref, v_ref, fk_ref, fv_ref, ka_ref, vt_ref):
    live = live_ref[0]
    slots, width = k_ref.shape
    fresh = fk_ref.shape[0]
    step = 256
    first = k_ref[0:16, :].astype(F32)[0:1, :]
    for at in range(0, slots, step):
        alive = lax.broadcasted_iota(jnp.int32, (step, width), 0) + at < live
        keys = jnp.where(alive, k_ref[at : at + step, :].astype(F32), first)
        ka_ref[at : at + step, :] = keys.astype(BF)
        vals = jnp.where(alive, v_ref[at : at + step, :].astype(F32), 0.0)
        vt_ref[0:width, at : at + step] = vals.T.astype(BF)
        flags = lax.broadcasted_iota(jnp.int32, (16, step), 1) + at < live
        vt_ref[width:, at : at + step] = flags.astype(F32).astype(BF)
    keys = jnp.concatenate([fk_ref[...].astype(F32), jnp.zeros((16 - fresh, width), F32)], 0)
    ka_ref[slots:, :] = keys.astype(BF)
    vals = jnp.concatenate([fv_ref[...].astype(F32), jnp.zeros((128 - fresh, width), F32)], 0)
    vt_ref[0:width, slots:] = vals.T.astype(BF)
    flags = lax.broadcasted_iota(jnp.int32, (16, 128), 1) < fresh
    vt_ref[width:, slots:] = flags.astype(F32).astype(BF)


def prepare(live, keys, vals, fresh_k, fresh_v):
    slots, width = keys.shape
    out = [
        jax.ShapeDtypeStruct((slots + 16, width), BF),
        jax.ShapeDtypeStruct((width + 16, slots + 128), BF),
    ]
    return call(prepare_body, out, smem=1, args=(live, keys, vals, fresh_k, fresh_v))


def three(value):
    parts = []
    for _ in range(3):
        top = value.astype(BF).astype(F32)
        parts.append(top)
        value = value - top
    return parts


def attend_body(step, place_ref, seg_ref, ka_ref, vt_ref, q_ref, o_ref, qt_ref, lse_ref, worst_ref):
    keys, width = ka_ref.shape
    slots = keys - 16
    rows = 256
    heads = 16
    fresh = 4
    pieces = q_ref.shape[0] // rows
    factor = LOG2E / width**0.5
    y, z = place_ref[0], place_ref[1]
    first = fresh * (SIDE * y + z)
    line = lax.broadcasted_iota(jnp.int32, (16, rows), 0)
    never = 1 << 30
    opens = jnp.where(line < fresh, line + first, never)
    ends = jnp.full((16, rows), never, jnp.int32)
    seg = seg_ref[...]
    spot = lax.broadcasted_iota(jnp.int32, seg.shape, 0) * 128 + lax.broadcasted_iota(
        jnp.int32, seg.shape, 1
    )
    for j in range(fresh):
        own = jnp.sum(jnp.where(spot == first + j, seg, 0))
        ends = jnp.where(line == j, jnp.sum((seg <= own).astype(jnp.int32)), ends)
    lane = lax.broadcasted_iota(jnp.int32, (16, rows), 1)
    which = coset(y - step[0], z - step[1])
    cuts = [(at, 256) for at in range(0, slots, 256)] + [(slots, 16)]

    for i in range(pieces):
        at = slice(i * rows, (i + 1) * rows)
        qt_ref[:, at] = q_ref[at, :].astype(F32).T.astype(BF)

    def score(query, cut, i):
        at, deep = cut
        part = jnp.dot(ka_ref[at : at + deep, :], query, preferred_element_type=F32)
        if deep == 16:
            member = 4 * i + lane // 64
            token = 32 * member_y(which, member) + 4 * (member // 2)
            token = token + lax.rem(lane // heads, 4)
            part = jnp.where((token >= opens) & (token < ends), part, -jnp.inf)
        return part

    def most(part):
        return jnp.max(part, axis=0, keepdims=True)

    def weigh(part, cut, peak, total):
        weight = jnp.exp2((part - peak) * factor).astype(BF)
        at, wide = cut
        if wide == 16:
            weight = jnp.concatenate([weight, jnp.zeros((112, rows), BF)], 0)
            wide = 128
        add = jnp.dot(vt_ref[:, at : at + wide], weight, preferred_element_type=F32)
        return add if total is None else total + add

    def finish(i, peak, total):
        count = total[width : width + 1, :]
        out = total[0:width, :] * (1.0 / count)
        at = i * rows
        if not isinstance(i, int):
            at = pl.multiple_of(at, rows)
        o_ref[pl.ds(at, rows), :] = out.T.astype(BF)
        lse = peak * factor + jnp.log(count) * LOG2E
        lse_ref[i] = jnp.concatenate([lse[:, 0:128], lse[:, 128:256]], 0)
        return count

    def query_of(i):
        return qt_ref[:, i * rows : (i + 1) * rows]

    worst = None
    todo = [(i, cut) for i in range(pieces) for cut in cuts]
    ahead = score(query_of(0), cuts[0], 0)
    peak_ahead = most(ahead)
    for n, (i, cut) in enumerate(todo):
        part, peak = ahead, peak_ahead
        if n + 1 < len(todo):
            j, later = todo[n + 1]
            ahead = score(query_of(j), later, j)
            if later == cuts[0]:
                peak_ahead = most(ahead)
        total = weigh(part, cut, peak, None if cut == cuts[0] else total)
        if cut == cuts[-1]:
            count = finish(i, peak, total)
            worst = count if worst is None else jnp.maximum(worst, count)
    worst_ref[...] = jnp.broadcast_to(worst, worst_ref.shape)

    @pl.when(jnp.logical_not(jnp.max(worst_ref[0:1, :]) < HUGE))
    def _():
        def slow(i, carry):
            at = pl.multiple_of(i * rows, rows)
            query = qt_ref[:, pl.ds(at, rows)]
            peak = None
            for cut in cuts:
                top = most(score(query, cut, i))
                peak = top if peak is None else jnp.maximum(peak, top)
            total = None
            for cut in cuts:
                total = weigh(score(query, cut, i), cut, peak, total)
            finish(i, peak, total)
            return carry

        lax.fori_loop(0, pieces, slow, 0)

    lse = jnp.concatenate([lse_ref[i] for i in range(pieces)], 0)
    parts = three(lse) + [jnp.zeros((8, 128), F32)]
    o_ref[pieces * rows :, :] = jnp.concatenate(parts, 0).astype(BF)


def attend(place, seg, ka, vt, query, step):
    rows, width = query.shape
    return call(
        functools.partial(attend_body, step),
        jax.ShapeDtypeStruct((rows + TAIL, width), BF),
        flops=8 * rows * ka.shape[0] * 256,
        moved=(ka.size + vt.size + 2 * query.size) * 2,
        scratch=[
            pltpu.VMEM((width, rows), BF),
            pltpu.VMEM((4, 2, 128), F32),
            pltpu.VMEM((8, 256), F32),
        ],
        smem=1,
        args=(place, seg, ka, vt, query),
    )


def diagonal(rows):
    return lax.broadcasted_iota(jnp.int32, (rows, 128), 0) == lax.broadcasted_iota(
        jnp.int32, (rows, 128), 1
    )


def spread(row, eye):
    return jnp.sum(jnp.where(eye, row, 0.0), axis=1, keepdims=True)


def first_body(*refs):
    ins, out_ref = refs[:-1], refs[-1]
    rows = ins[0].shape[0] - TAIL
    eye = diagonal(128)
    logs = []
    for ref in ins:
        tail = ref[rows:, :].astype(F32)
        logs.append(tail[0:8] + tail[8:16] + tail[16:24])
    top = functools.reduce(jnp.maximum, logs)
    weights = [jnp.exp2(log - top) for log in logs]
    total = functools.reduce(jnp.add, weights)
    lse = top + jnp.log(total) * LOG2E
    weights = [w / total for w in weights]
    parts = []
    for _ in range(3):
        high = lse.astype(BF).astype(F32)
        parts.append(high)
        lse = lse - high
    empty = jnp.zeros((5, 128), F32)
    for b in range(rows // 128):
        merged = None
        for ref, weight in zip(ins, weights):
            term = ref[b * 128 : (b + 1) * 128, :].astype(F32) * spread(weight[b : b + 1], eye)
            merged = term if merged is None else merged + term
        merged = merged.astype(BF)
        tail = jnp.concatenate([p[b : b + 1] for p in parts] + [empty], 0).astype(BF)
        for j in range(2):
            out_ref[2 * b + j, 0:64, :] = merged[64 * j : 64 * j + 64, :]
            out_ref[2 * b + j, 64:72, :] = tail


def first_merge(ins):
    rows, width = ins[0].shape
    out = jax.ShapeDtypeStruct(((rows - TAIL) // 64, 72, width), BF)
    return call(first_body, out, args=tuple(ins))


def second_body(place_ref, got_ref, out_ref, logs):
    parts = got_ref.shape[0]
    for c in range(parts):
        tail = got_ref[c, 64:72, :].astype(F32)
        logs[c : c + 1, :] = tail[0:1] + tail[1:2] + tail[2:3]
    lse = logs[...]
    lse = jnp.where(place_ref[0] // 4 == 1, pltpu.roll(lse, 64, 1), lse)
    weight = jnp.exp2(lse - jnp.max(lse, axis=0, keepdims=True))
    weight = weight / jnp.sum(weight, axis=0, keepdims=True)
    eye = diagonal(64)
    total = None
    for c in range(parts):
        term = got_ref[c, 0:64, :].astype(F32) * spread(weight[c : c + 1, :], eye)
        total = term if total is None else total + term
    out_ref[...] = total.astype(BF)


def second_merge(place, got):
    return call(
        second_body,
        jax.ShapeDtypeStruct((64, got.shape[2]), BF),
        scratch=[pltpu.VMEM((got.shape[0], 128), F32)],
        smem=1,
        args=(place, got),
    )


def project_body(w_ref, *refs):
    ins, out_ref, rows = refs[:2], refs[2], refs[3]
    heads = w_ref.shape[0] // ins[0].shape[1]
    tokens = ins[0].shape[0] // heads
    left = []
    for ref in ins:
        rows[...] = ref[...].astype(F32)
        parts = [rows[pl.ds(h, tokens, stride=heads), :].astype(BF) for h in range(heads)]
        left.append(jnp.concatenate(parts, 1))
    mixed = jnp.dot(jnp.concatenate(left, 0), w_ref[...], preferred_element_type=F32)
    for k in range(out_ref.shape[0]):
        for i in range(2):
            at = i * tokens + 16 * k
            out_ref[k, 16 * i : 16 * i + 16, :] = mixed[at : at + 16, :].astype(BF)


def project(weight, ins):
    deep, cols = weight.shape
    rows, width = ins[0].shape
    tokens = 2 * rows * width // deep
    return call(
        project_body,
        jax.ShapeDtypeStruct((8, tokens // 8, cols), BF),
        flops=2 * tokens * deep * cols,
        scratch=[pltpu.VMEM((rows, width), F32)],
        args=(weight, *ins),
    )


def final_body(got_ref, out_ref):
    total = got_ref[0].astype(F32)
    for i in range(1, got_ref.shape[0]):
        total = total + got_ref[i].astype(F32)
    out_ref[...] = total.astype(BF)


def along(value, axis):
    lines = [[y * SIDE + z for z in range(SIDE)] for y in range(SIDE)]
    if axis == "y":
        lines = [list(line) for line in zip(*lines)]
    return lax.all_gather(value, "ctx", axis=0, tiled=True, axis_index_groups=lines)


def local(queries, cache_keys, cache_values, new_keys, new_values, cache_len, segment, out_weight):
    me = lax.axis_index("ctx").astype(jnp.int32)
    place = jnp.stack([me // SIDE, me % SIDE])
    block, heads, width = queries.shape
    ka, vt = prepare(
        cache_len,
        cache_keys[:, 0, :],
        cache_values[:, 0, :],
        new_keys[:, 0, :],
        new_values[:, 0, :],
    )
    mine = share(queries.reshape(block * heads, width))
    asked = [mine] + [shift(mine, step) for step in STEPS[1:]]
    seg = segment.reshape(-1, 128)
    partial = [attend(place, seg, ka, vt, q, step) for q, step in zip(asked, STEPS)]
    back = [shift(p, (-s[0], -s[1])) for p, s in zip(partial[1:], STEPS[1:])]
    own = second_merge(place, exchange(first_merge([partial[0]] + back)))
    line = along(own, "z")
    half = line.shape[0] // 2
    mixed = project(out_weight, [along(line[:half], "y"), along(line[half:], "y")])
    got = lax.all_to_all(mixed, "kvh", 0, 0, tiled=True)
    return call(final_body, jax.ShapeDtypeStruct(got.shape[1:], BF), args=(got,))


def solution(mesh):
    in_specs = (
        P("ctx", "kvh", None),
        P("ctx", "kvh", None),
        P("ctx", "kvh", None),
        P("ctx", "kvh", None),
        P("ctx", "kvh", None),
        P("ctx"),
        P(),
        P("kvh", "ctx"),
    )
    out_specs = P("kvh", "ctx")
    return jax.shard_map(local, mesh=mesh, in_specs=in_specs, out_specs=out_specs, check_vma=False)
```

```python
import functools

import jax
import jax.numpy as jnp
from jax import lax
from jax.experimental import pallas as pl
from jax.experimental.pallas import tpu as pltpu
from jax.sharding import PartitionSpec as P

BF = jnp.bfloat16
F32 = jnp.float32
LOG2E = 1.4426950408889634
LIMIT = 48 * 1024 * 1024
HUGE = 2.0**100
SIDE = 8
STEPS = ((0, 0), (1, 0), (-1, 0), (0, 1))
TAIL = 32


def shift(value, step):
    pairs = []
    for y in range(SIDE):
        for z in range(SIDE):
            to = ((y + step[0]) % SIDE) * SIDE + (z + step[1]) % SIDE
            pairs.append((y * SIDE + z, to))
    return lax.ppermute(value, "ctx", pairs)


def coset(y, z):
    return lax.rem(y + 2 * z + 4 * SIDE, 4)


def member_y(which, i):
    return lax.rem(which + 2 * (i // 2), 4) + 4 * (i % 2)


def cosets():
    return [
        [((v + 2 * z) % 4 + 4 * b) * SIDE + z for z in range(SIDE) for b in range(2)]
        for v in range(4)
    ]


def exchange(value):
    return lax.all_to_all(value, "ctx", 0, 0, axis_index_groups=cosets(), tiled=True)


def share(value):
    copies = jnp.broadcast_to(value[None], (16,) + value.shape)
    return exchange(copies).reshape(16 * value.shape[0], value.shape[1])


def call(body, out_shape, flops=0, moved=0, scratch=(), smem=0, args=()):
    vmem = pl.BlockSpec(memory_space=pltpu.VMEM)
    scalars = pl.BlockSpec(memory_space=pltpu.SMEM)
    specs = [scalars] * smem + [vmem] * (len(args) - smem)
    return pl.pallas_call(
        body,
        out_shape=out_shape,
        in_specs=specs,
        out_specs=jax.tree.map(lambda _: vmem, out_shape),
        scratch_shapes=list(scratch),
        compiler_params=pltpu.CompilerParams(vmem_limit_bytes=LIMIT),
        cost_estimate=pl.CostEstimate(flops=flops, bytes_accessed=moved, transcendentals=0),
    )(*args)


def prepare_body(live_ref, place_ref, seg_ref, k_ref, v_ref, fk_ref, fv_ref, ka_ref, vt_ref, b_ref):
    live = live_ref[0]
    slots, width = k_ref.shape
    fresh = fk_ref.shape[0]
    step = 256
    first = k_ref[0:16, :].astype(F32)[0:1, :]
    for at in range(0, slots, step):
        alive = lax.broadcasted_iota(jnp.int32, (step, width), 0) + at < live
        keys = jnp.where(alive, k_ref[at : at + step, :].astype(F32), first)
        ka_ref[at : at + step, :] = keys.astype(BF)
        vals = jnp.where(alive, v_ref[at : at + step, :].astype(F32), 0.0)
        vt_ref[0:width, at : at + step] = vals.T.astype(BF)
        flags = lax.broadcasted_iota(jnp.int32, (16, step), 1) + at < live
        vt_ref[width:, at : at + step] = flags.astype(F32).astype(BF)
    keys = jnp.concatenate([fk_ref[...].astype(F32), jnp.zeros((16 - fresh, width), F32)], 0)
    ka_ref[slots:, :] = keys.astype(BF)
    vals = jnp.concatenate([fv_ref[...].astype(F32), jnp.zeros((128 - fresh, width), F32)], 0)
    vt_ref[0:width, slots:] = vals.T.astype(BF)
    flags = lax.broadcasted_iota(jnp.int32, (16, 128), 1) < fresh
    vt_ref[width:, slots:] = flags.astype(F32).astype(BF)
    mine = fresh * (SIDE * place_ref[0] + place_ref[1])
    line = lax.broadcasted_iota(jnp.int32, (16, 128), 0)
    never = 1 << 30
    ends = jnp.full((16, 128), never, jnp.int32)
    seg = seg_ref[...]
    spot = lax.broadcasted_iota(jnp.int32, seg.shape, 0) * 128 + lax.broadcasted_iota(
        jnp.int32, seg.shape, 1
    )
    for j in range(fresh):
        own = jnp.sum(jnp.where(spot == mine + j, seg, 0))
        ends = jnp.where(line == j, jnp.sum((seg <= own).astype(jnp.int32)), ends)
    b_ref[0:16, :] = jnp.where(line < fresh, line + mine, never)
    b_ref[16:32, :] = ends


def prepare(live, place, seg, keys, vals, fresh_k, fresh_v):
    slots, width = keys.shape
    out = [
        jax.ShapeDtypeStruct((slots + 16, width), BF),
        jax.ShapeDtypeStruct((width + 16, slots + 128), BF),
        jax.ShapeDtypeStruct((32, 128), jnp.int32),
    ]
    args = (live, place, seg, keys, vals, fresh_k, fresh_v)
    return call(prepare_body, out, smem=2, args=args)


def turn_body(bound_ref, q_ref, out_ref):
    for at in range(0, q_ref.shape[0], 256):
        out_ref[:, at : at + 256] = q_ref[at : at + 256, :].astype(F32).T.astype(BF)


def turn(bounds, query):
    out = jax.ShapeDtypeStruct(query.shape[::-1], BF)
    return call(turn_body, out, args=(bounds, query))


def three(value):
    parts = []
    for _ in range(3):
        top = value.astype(BF).astype(F32)
        parts.append(top)
        value = value - top
    return parts


def attend_body(step, place_ref, bound_ref, ka_ref, vt_ref, qt_ref, o_ref, lse_ref, worst_ref):
    keys, width = ka_ref.shape
    slots = keys - 16
    rows = 256
    heads = 16
    pieces = qt_ref.shape[1] // rows
    factor = LOG2E / width**0.5
    opens = jnp.concatenate([bound_ref[0:16, :]] * 2, 1)
    ends = jnp.concatenate([bound_ref[16:32, :]] * 2, 1)
    lane = lax.broadcasted_iota(jnp.int32, (16, rows), 1)
    which = coset(place_ref[0] - step[0], place_ref[1] - step[1])
    cuts = [(at, 256) for at in range(0, slots, 256)] + [(slots, 16)]

    def score(query, cut, i):
        at, deep = cut
        part = jnp.dot(ka_ref[at : at + deep, :], query, preferred_element_type=F32)
        if deep == 16:
            member = 4 * i + lane // 64
            token = 32 * member_y(which, member) + 4 * (member // 2)
            token = token + lax.rem(lane // heads, 4)
            part = jnp.where((token >= opens) & (token < ends), part, -jnp.inf)
        return part

    def most(part):
        return jnp.max(part, axis=0, keepdims=True)

    def weigh(part, cut, peak, total):
        weight = jnp.exp2((part - peak) * factor).astype(BF)
        at, wide = cut
        if wide == 16:
            weight = jnp.concatenate([weight, jnp.zeros((112, rows), BF)], 0)
            wide = 128
        add = jnp.dot(vt_ref[:, at : at + wide], weight, preferred_element_type=F32)
        return add if total is None else total + add

    def finish(i, peak, total):
        count = total[width : width + 1, :]
        out = total[0:width, :] * (1.0 / count)
        at = i * rows
        if not isinstance(i, int):
            at = pl.multiple_of(at, rows)
        o_ref[pl.ds(at, rows), :] = out.T.astype(BF)
        lse = peak * factor + jnp.log(count) * LOG2E
        lse_ref[i] = jnp.concatenate([lse[:, 0:128], lse[:, 128:256]], 0)
        return count

    def query_of(i):
        return qt_ref[:, i * rows : (i + 1) * rows]

    worst = None
    todo = [(i, cut) for i in range(pieces) for cut in cuts]
    ahead = score(query_of(0), cuts[0], 0)
    peak_ahead = most(ahead)
    for n, (i, cut) in enumerate(todo):
        part, peak = ahead, peak_ahead
        if n + 1 < len(todo):
            j, later = todo[n + 1]
            ahead = score(query_of(j), later, j)
            if later == cuts[0]:
                peak_ahead = most(ahead)
        total = weigh(part, cut, peak, None if cut == cuts[0] else total)
        if cut == cuts[-1]:
            count = finish(i, peak, total)
            worst = count if worst is None else jnp.maximum(worst, count)
    worst_ref[...] = jnp.broadcast_to(worst, worst_ref.shape)

    @pl.when(jnp.logical_not(jnp.max(worst_ref[0:1, :]) < HUGE))
    def _():
        def slow(i, carry):
            at = pl.multiple_of(i * rows, rows)
            query = qt_ref[:, pl.ds(at, rows)]
            peak = None
            for cut in cuts:
                top = most(score(query, cut, i))
                peak = top if peak is None else jnp.maximum(peak, top)
            total = None
            for cut in cuts:
                total = weigh(score(query, cut, i), cut, peak, total)
            finish(i, peak, total)
            return carry

        lax.fori_loop(0, pieces, slow, 0)

    lse = jnp.concatenate([lse_ref[i] for i in range(pieces)], 0)
    parts = three(lse) + [jnp.zeros((8, 128), F32)]
    o_ref[pieces * rows :, :] = jnp.concatenate(parts, 0).astype(BF)


def attend(place, bounds, ka, vt, query, step):
    width, rows = query.shape
    return call(
        functools.partial(attend_body, step),
        jax.ShapeDtypeStruct((rows + TAIL, width), BF),
        flops=8 * rows * ka.shape[0] * 256,
        moved=(ka.size + vt.size + 2 * query.size) * 2,
        scratch=[pltpu.VMEM((4, 2, 128), F32), pltpu.VMEM((8, 256), F32)],
        smem=1,
        args=(place, bounds, ka, vt, query),
    )


def diagonal(rows):
    return lax.broadcasted_iota(jnp.int32, (rows, 128), 0) == lax.broadcasted_iota(
        jnp.int32, (rows, 128), 1
    )


def spread(row, eye):
    return jnp.sum(jnp.where(eye, row, 0.0), axis=1, keepdims=True)


def first_body(*refs):
    ins, out_ref = refs[:-1], refs[-1]
    rows = ins[0].shape[0] - TAIL
    eye = diagonal(128)
    logs = []
    for ref in ins:
        tail = ref[rows:, :].astype(F32)
        logs.append(tail[0:8] + tail[8:16] + tail[16:24])
    top = functools.reduce(jnp.maximum, logs)
    weights = [jnp.exp2(log - top) for log in logs]
    total = functools.reduce(jnp.add, weights)
    lse = top + jnp.log(total) * LOG2E
    weights = [w / total for w in weights]
    parts = []
    for _ in range(3):
        high = lse.astype(BF).astype(F32)
        parts.append(high)
        lse = lse - high
    empty = jnp.zeros((5, 128), F32)
    for b in range(rows // 128):
        merged = None
        for ref, weight in zip(ins, weights):
            term = ref[b * 128 : (b + 1) * 128, :].astype(F32) * spread(weight[b : b + 1], eye)
            merged = term if merged is None else merged + term
        merged = merged.astype(BF)
        tail = jnp.concatenate([p[b : b + 1] for p in parts] + [empty], 0).astype(BF)
        for j in range(2):
            out_ref[2 * b + j, 0:64, :] = merged[64 * j : 64 * j + 64, :]
            out_ref[2 * b + j, 64:72, :] = tail


def first_merge(ins):
    rows, width = ins[0].shape
    out = jax.ShapeDtypeStruct(((rows - TAIL) // 64, 72, width), BF)
    return call(first_body, out, args=tuple(ins))


def second_body(place_ref, got_ref, out_ref, logs):
    parts = got_ref.shape[0]
    for c in range(parts):
        tail = got_ref[c, 64:72, :].astype(F32)
        logs[c : c + 1, :] = tail[0:1] + tail[1:2] + tail[2:3]
    lse = logs[...]
    lse = jnp.where(place_ref[0] // 4 == 1, pltpu.roll(lse, 64, 1), lse)
    weight = jnp.exp2(lse - jnp.max(lse, axis=0, keepdims=True))
    weight = weight / jnp.sum(weight, axis=0, keepdims=True)
    eye = diagonal(64)
    total = None
    for c in range(parts):
        term = got_ref[c, 0:64, :].astype(F32) * spread(weight[c : c + 1, :], eye)
        total = term if total is None else total + term
    out_ref[...] = total.astype(BF)


def second_merge(place, got):
    return call(
        second_body,
        jax.ShapeDtypeStruct((64, got.shape[2]), BF),
        scratch=[pltpu.VMEM((got.shape[0], 128), F32)],
        smem=1,
        args=(place, got),
    )


def project_body(place_ref, w_ref, *refs):
    ins, out_ref, rows = refs[:4], refs[4], refs[5]
    heads = w_ref.shape[0] // ins[0].shape[1]
    tokens = rows.shape[0] // heads
    for ref, step in zip(ins, STEPS):
        which = coset(place_ref[0] - step[0], place_ref[1] - step[1])
        for n in range(ref.shape[0] // 64):
            to = pl.multiple_of(64 * (SIDE * member_y(which, n) + n // 2), 64)
            rows[pl.ds(to, 64), :] = ref[64 * n : 64 * n + 64, :].astype(F32)
    left = [rows[pl.ds(h, tokens, stride=heads), :].astype(BF) for h in range(heads)]
    mixed = jnp.dot(jnp.concatenate(left, 1), w_ref[...], preferred_element_type=F32)
    out_ref[...] = mixed.astype(BF)


def project(place, weight, ins):
    deep, cols = weight.shape
    rows, width = ins[0].shape
    tokens = 4 * rows * width // deep
    return call(
        project_body,
        jax.ShapeDtypeStruct((tokens, cols), BF),
        flops=2 * tokens * deep * cols,
        scratch=[pltpu.VMEM((4 * rows, width), F32)],
        smem=1,
        args=(place, weight, *ins),
    )


def final_body(got_ref, out_ref):
    total = got_ref[0].astype(F32)
    for i in range(1, got_ref.shape[0]):
        total = total + got_ref[i].astype(F32)
    out_ref[...] = total.astype(BF)


def local(queries, cache_keys, cache_values, new_keys, new_values, cache_len, segment, out_weight):
    me = lax.axis_index("ctx").astype(jnp.int32)
    place = jnp.stack([me // SIDE, me % SIDE])
    block, heads, width = queries.shape
    ka, vt, bounds = prepare(
        cache_len,
        place,
        segment.reshape(-1, 128),
        cache_keys[:, 0, :],
        cache_values[:, 0, :],
        new_keys[:, 0, :],
        new_values[:, 0, :],
    )
    mine = turn(bounds, share(queries.reshape(block * heads, width)))
    asked = [mine] + [shift(mine, step) for step in STEPS[1:]]
    partial = [attend(place, bounds, ka, vt, q, step) for q, step in zip(asked, STEPS)]
    back = [shift(p, (-s[0], -s[1])) for p, s in zip(partial[1:], STEPS[1:])]
    own = second_merge(place, exchange(first_merge([partial[0]] + back)))
    mine = share(own)
    every = [mine] + [shift(mine, step) for step in STEPS[1:]]
    mixed = project(place, out_weight, every)
    mixed = mixed.reshape(lax.axis_size("kvh"), -1, mixed.shape[1])
    got = lax.all_to_all(mixed, "kvh", 0, 0, tiled=True)
    return call(final_body, jax.ShapeDtypeStruct(got.shape[1:], BF), args=(got,))


def solution(mesh):
    in_specs = (
        P("ctx", "kvh", None),
        P("ctx", "kvh", None),
        P("ctx", "kvh", None),
        P("ctx", "kvh", None),
        P("ctx", "kvh", None),
        P("ctx"),
        P(),
        P("kvh", "ctx"),
    )
    out_specs = P("kvh", "ctx")
    return jax.shard_map(local, mesh=mesh, in_specs=in_specs, out_specs=out_specs, check_vma=False)
```

```python
import functools

import jax
import jax.numpy as jnp
from jax import lax
from jax.experimental import pallas as pl
from jax.experimental.pallas import tpu as pltpu
from jax.sharding import PartitionSpec as P

BF = jnp.bfloat16
F32 = jnp.float32
LOG2E = 1.4426950408889634
LIMIT = 48 * 1024 * 1024
HUGE = 2.0**100
SIDE = 8
STEPS = ((0, 0), (1, 0), (-1, 0), (0, 1))
TAIL = 32


def shift(value, step):
    pairs = []
    for y in range(SIDE):
        for z in range(SIDE):
            to = ((y + step[0]) % SIDE) * SIDE + (z + step[1]) % SIDE
            pairs.append((y * SIDE + z, to))
    return lax.ppermute(value, "ctx", pairs)


def coset(y, z):
    return lax.rem(y + 2 * z + 4 * SIDE, 4)


def member_y(which, i):
    return lax.rem(which + 2 * (i // 2), 4) + 4 * (i % 2)


def cosets():
    return [
        [((v + 2 * z) % 4 + 4 * b) * SIDE + z for z in range(SIDE) for b in range(2)]
        for v in range(4)
    ]


def exchange(value):
    return lax.all_to_all(value, "ctx", 0, 0, axis_index_groups=cosets(), tiled=True)


def share(value):
    copies = jnp.broadcast_to(value[None], (16,) + value.shape)
    return exchange(copies).reshape(16 * value.shape[0], value.shape[1])


def call(body, out_shape, flops=0, moved=0, scratch=(), smem=0, args=()):
    vmem = pl.BlockSpec(memory_space=pltpu.VMEM)
    scalars = pl.BlockSpec(memory_space=pltpu.SMEM)
    specs = [scalars] * smem + [vmem] * (len(args) - smem)
    return pl.pallas_call(
        body,
        out_shape=out_shape,
        in_specs=specs,
        out_specs=jax.tree.map(lambda _: vmem, out_shape),
        scratch_shapes=list(scratch),
        compiler_params=pltpu.CompilerParams(vmem_limit_bytes=LIMIT),
        cost_estimate=pl.CostEstimate(flops=flops, bytes_accessed=moved, transcendentals=0),
    )(*args)


def turned(kv_ref, span, fresh, live, vt_ref):
    width = kv_ref.shape[1]
    slots = span - fresh
    step = 256
    for at in range(0, slots, step):
        vals = kv_ref[span + at : span + at + step, :].astype(F32)
        vt_ref[0:width, at : at + step] = vals.T.astype(BF)
        flags = lax.broadcasted_iota(jnp.int32, (16, step), 1) + at < live
        vt_ref[width:, at : at + step] = flags.astype(F32).astype(BF)
    if fresh:
        vals = kv_ref[span + slots : 2 * span, :].astype(F32)
        vals = jnp.concatenate([vals, jnp.zeros((128 - fresh, width), F32)], 0)
        vt_ref[0:width, slots:] = vals.T.astype(BF)
        flags = lax.broadcasted_iota(jnp.int32, (16, 128), 1) < 4
        vt_ref[width:, slots:] = flags.astype(F32).astype(BF)


def bounds_of(first, seg, live, b_ref):
    line = lax.broadcasted_iota(jnp.int32, (16, 128), 0)
    never = 1 << 30
    ends = jnp.full((16, 128), never, jnp.int32)
    spot = lax.broadcasted_iota(jnp.int32, seg.shape, 0) * 128 + lax.broadcasted_iota(
        jnp.int32, seg.shape, 1
    )
    for j in range(4):
        own = jnp.sum(jnp.where(spot == first + j, seg, 0))
        ends = jnp.where(line == j, jnp.sum((seg <= own).astype(jnp.int32)), ends)
    b_ref[0:16, :] = jnp.where(line < 4, line + first, never)
    b_ref[16:32, :] = ends
    b_ref[32:40, :] = jnp.zeros((8, 128), jnp.int32) + live


def prepare_body(live_ref, place_ref, seg_ref, k_ref, v_ref, fk_ref, fv_ref, *outs):
    live = live_ref[0]
    slots, width = k_ref.shape
    half = slots // 2
    step = 256
    first = k_ref[0:16, :].astype(F32)[0:1, :]
    line = lax.broadcasted_iota(jnp.int32, (16, width), 0)
    size = jnp.where(line == 0, live // 64, jnp.where(line == 1, lax.rem(live, 64), 0))
    pad = jnp.zeros((16 - fk_ref.shape[0], width), F32)
    for n in range(2):
        kv_ref, vt_ref, b_ref = outs[3 * n : 3 * n + 3]
        fresh = 16 * n
        span = half + fresh
        for at in range(0, half, step):
            rows = slice(n * half + at, n * half + at + step)
            alive = lax.broadcasted_iota(jnp.int32, (step, width), 0) + n * half + at < live
            keys = jnp.where(alive, k_ref[rows, :].astype(F32), first)
            kv_ref[at : at + step, :] = keys.astype(BF)
            vals = jnp.where(alive, v_ref[rows, :].astype(F32), 0.0)
            kv_ref[span + at : span + at + step, :] = vals.astype(BF)
        if fresh:
            for at, ref in ((half, fk_ref), (span + half, fv_ref)):
                new = jnp.concatenate([ref[...].astype(F32), pad], 0)
                kv_ref[at : at + 16, :] = new.astype(BF)
        kv_ref[2 * span :, :] = size.astype(F32).astype(BF)
        turned(kv_ref, span, fresh, live - n * half, vt_ref)
        first_token = 4 * (SIDE * place_ref[0] + place_ref[1])
        bounds_of(first_token, seg_ref[...], live - n * half, b_ref)


def ready_shapes(half, n, width):
    return [
        jax.ShapeDtypeStruct((width + 16, half + 128 * n), BF),
        jax.ShapeDtypeStruct((40, 128), jnp.int32),
    ]


def prepare(live, place, seg, keys, vals, fresh_k, fresh_v):
    slots, width = keys.shape
    half = slots // 2
    out = []
    for n in range(2):
        out.append(jax.ShapeDtypeStruct((2 * (half + 16 * n) + 16, width), BF))
        out += ready_shapes(half, n, width)
    args = (live, place, seg, keys, vals, fresh_k, fresh_v)
    got = call(prepare_body, out, smem=2, args=args)
    return tuple(got[:3]), tuple(got[3:])


def unpack_body(place_ref, seg_ref, lower_ref, upper_ref, *outs):
    for n, kv_ref in enumerate((lower_ref, upper_ref)):
        vt_ref, b_ref = outs[2 * n : 2 * n + 2]
        span = (kv_ref.shape[0] - 16) // 2
        fresh = 16 * n
        size = kv_ref[2 * span :, :].astype(F32)
        live = jnp.max(64.0 * size[0:1] + size[1:2]).astype(jnp.int32)
        live = live - n * (span - fresh)
        turned(kv_ref, span, fresh, live, vt_ref)
        from_z = lax.rem(place_ref[1] + SIDE - 1 + 2 * n, SIDE)
        bounds_of(4 * (SIDE * place_ref[0] + from_z), seg_ref[...], live, b_ref)


def unpack(place, seg, lower, upper):
    half, width = (lower.shape[0] - 16) // 2, lower.shape[1]
    out = ready_shapes(half, 0, width) + ready_shapes(half, 1, width)
    got = call(unpack_body, out, smem=1, args=(place, seg, lower, upper))
    return (lower, *got[:2]), (upper, *got[2:])


def turn_body(bound_ref, q_ref, out_ref):
    for at in range(0, q_ref.shape[0], 256):
        out_ref[:, at : at + 256] = q_ref[at : at + 256, :].astype(F32).T.astype(BF)


def turn(bounds, query):
    out = jax.ShapeDtypeStruct(query.shape[::-1], BF)
    return call(turn_body, out, args=(bounds, query))


def three(value):
    parts = []
    for _ in range(3):
        top = value.astype(BF).astype(F32)
        parts.append(top)
        value = value - top
    return parts


def attend_body(step, begin, place_ref, qt_ref, *refs):
    count = 2 if begin else 4
    shards = [refs[3 * n : 3 * n + 3] for n in range(count)]
    if begin:
        acc_out, peak_out = refs[6:]
    else:
        acc_in, peak_in, o_ref, lse_ref, worst_ref = refs[12:]
    width = qt_ref.shape[0]
    slots = shards[0][1].shape[1]
    rows = 256
    heads = 16
    pieces = qt_ref.shape[1] // rows
    factor = LOG2E / width**0.5
    lane = lax.broadcasted_iota(jnp.int32, (16, rows), 1)
    which = coset(place_ref[0] - step[0], place_ref[1] - step[1])

    def cuts_of(n):
        return [(n, at, 256) for at in range(0, slots, 256)] + [(n, slots, 16)] * (n % 2)

    def score(query, cut, i, exact=False):
        n, at, deep = cut
        kv_ref, vt_ref, b_ref = shards[n]
        part = jnp.dot(kv_ref[at : at + deep, :], query, preferred_element_type=F32)
        if deep == 16:
            opens = jnp.concatenate([b_ref[0:16, :]] * 2, 1)
            ends = jnp.concatenate([b_ref[16:32, :]] * 2, 1)
            member = 4 * i + lane // 64
            token = 32 * member_y(which, member) + 4 * (member // 2)
            token = token + lax.rem(lane // heads, 4)
            part = jnp.where((token >= opens) & (token < ends), part, -jnp.inf)
        elif exact:
            live = jnp.concatenate([b_ref[32:33, :]] * 2, 1)
            alive = lax.broadcasted_iota(jnp.int32, (deep, rows), 0) + at < live
            part = jnp.where(alive, part, -jnp.inf)
        return part

    def most(part):
        return jnp.max(part, axis=0, keepdims=True)

    def weigh(part, cut, peak, total):
        weight = jnp.exp2((part - peak) * factor).astype(BF)
        n, at, wide = cut
        if wide == 16:
            weight = jnp.concatenate([weight, jnp.zeros((112, rows), BF)], 0)
            wide = 128
        add = jnp.dot(shards[n][1][:, at : at + wide], weight, preferred_element_type=F32)
        return add if total is None else total + add

    def finish(i, peak, total):
        count = total[width : width + 1, :]
        out = total[0:width, :] * (1.0 / count)
        at = i * rows
        if not isinstance(i, int):
            at = pl.multiple_of(at, rows)
        o_ref[pl.ds(at, rows), :] = out.T.astype(BF)
        lse = peak * factor + jnp.log(count) * LOG2E
        lse_ref[i] = jnp.concatenate([lse[:, 0:128], lse[:, 128:256]], 0)
        return count

    def query_of(i):
        return qt_ref[:, i * rows : (i + 1) * rows]

    cuts = cuts_of(count - 2) + cuts_of(count - 1)
    worst = None
    todo = [(i, cut) for i in range(pieces) for cut in cuts]
    ahead = score(query_of(0), cuts[0], 0)
    peak_ahead = most(ahead)
    for at_todo, (i, cut) in enumerate(todo):
        part, at = ahead, slice(i * rows, (i + 1) * rows)
        if cut == cuts[0]:
            peak = peak_ahead if begin else peak_in[0:1, at]
            total = None if begin else acc_in[:, at]
        if at_todo + 1 < len(todo):
            j, later = todo[at_todo + 1]
            ahead = score(query_of(j), later, j)
            if begin and later == cuts[0]:
                peak_ahead = most(ahead)
        total = weigh(part, cut, peak, total)
        if cut == cuts[-1]:
            if begin:
                acc_out[:, at] = total
                peak_out[:, at] = jnp.broadcast_to(peak, (8, rows))
            else:
                counts = finish(i, peak, total)
                worst = counts if worst is None else jnp.maximum(worst, counts)
    if begin:
        return
    worst_ref[...] = jnp.broadcast_to(worst, worst_ref.shape)

    @pl.when(jnp.logical_not(jnp.max(worst_ref[0:1, :]) < HUGE))
    def _():
        def slow(i, carry):
            query = qt_ref[:, pl.ds(pl.multiple_of(i * rows, rows), rows)]
            peak, total = None, None
            every = sum((cuts_of(n) for n in range(count)), [])
            for cut in every:
                top = most(score(query, cut, i, True))
                peak = top if peak is None else jnp.maximum(peak, top)
            for cut in every:
                total = weigh(score(query, cut, i, True), cut, peak, total)
            finish(i, peak, total)
            return carry

        lax.fori_loop(0, pieces, slow, 0)

    lse = jnp.concatenate([lse_ref[i] for i in range(pieces)], 0)
    parts = three(lse) + [jnp.zeros((8, 128), F32)]
    o_ref[pieces * rows :, :] = jnp.concatenate(parts, 0).astype(BF)


def attend(place, query, near, step):
    width, rows = query.shape
    return call(
        functools.partial(attend_body, step, True),
        [
            jax.ShapeDtypeStruct((width + 16, rows), F32),
            jax.ShapeDtypeStruct((8, rows), F32),
        ],
        flops=8 * rows * near[0][1].shape[1] * 256,
        moved=8 * near[0][0].size,
        smem=1,
        args=(place, query, *near[0], *near[1]),
    )


def attend_on(place, query, near, far, sums, step):
    width, rows = query.shape
    return call(
        functools.partial(attend_body, step, False),
        jax.ShapeDtypeStruct((rows + TAIL, width), BF),
        flops=8 * rows * far[0][1].shape[1] * 256,
        moved=8 * far[0][0].size,
        scratch=[pltpu.VMEM((4, 2, 128), F32), pltpu.VMEM((8, 256), F32)],
        smem=1,
        args=(place, query, *near[0], *near[1], *far[0], *far[1], *sums),
    )


def diagonal(rows):
    return lax.broadcasted_iota(jnp.int32, (rows, 128), 0) == lax.broadcasted_iota(
        jnp.int32, (rows, 128), 1
    )


def spread(row, eye):
    return jnp.sum(jnp.where(eye, row, 0.0), axis=1, keepdims=True)


def first_body(*refs):
    ins, out_ref = refs[:-1], refs[-1]
    rows = ins[0].shape[0] - TAIL
    eye = diagonal(128)
    logs = []
    for ref in ins:
        tail = ref[rows:, :].astype(F32)
        logs.append(tail[0:8] + tail[8:16] + tail[16:24])
    top = functools.reduce(jnp.maximum, logs)
    weights = [jnp.exp2(log - top) for log in logs]
    total = functools.reduce(jnp.add, weights)
    lse = top + jnp.log(total) * LOG2E
    weights = [w / total for w in weights]
    parts = []
    for _ in range(3):
        high = lse.astype(BF).astype(F32)
        parts.append(high)
        lse = lse - high
    empty = jnp.zeros((5, 128), F32)
    for b in range(rows // 128):
        merged = None
        for ref, weight in zip(ins, weights):
            term = ref[b * 128 : (b + 1) * 128, :].astype(F32) * spread(weight[b : b + 1], eye)
            merged = term if merged is None else merged + term
        merged = merged.astype(BF)
        tail = jnp.concatenate([p[b : b + 1] for p in parts] + [empty], 0).astype(BF)
        for j in range(2):
            out_ref[2 * b + j, 0:64, :] = merged[64 * j : 64 * j + 64, :]
            out_ref[2 * b + j, 64:72, :] = tail


def first_merge(ins):
    rows, width = ins[0].shape
    out = jax.ShapeDtypeStruct(((rows - TAIL) // 64, 72, width), BF)
    return call(first_body, out, args=tuple(ins))


def second_body(place_ref, got_ref, out_ref, logs):
    parts = got_ref.shape[0]
    for c in range(parts):
        tail = got_ref[c, 64:72, :].astype(F32)
        logs[c : c + 1, :] = tail[0:1] + tail[1:2] + tail[2:3]
    lse = logs[...]
    lse = jnp.where(place_ref[0] // 4 == 1, pltpu.roll(lse, 64, 1), lse)
    weight = jnp.exp2(lse - jnp.max(lse, axis=0, keepdims=True))
    weight = weight / jnp.sum(weight, axis=0, keepdims=True)
    eye = diagonal(64)
    total = None
    for c in range(parts):
        term = got_ref[c, 0:64, :].astype(F32) * spread(weight[c : c + 1, :], eye)
        total = term if total is None else total + term
    out_ref[...] = total.astype(BF)


def second_merge(place, got):
    return call(
        second_body,
        jax.ShapeDtypeStruct((64, got.shape[2]), BF),
        scratch=[pltpu.VMEM((got.shape[0], 128), F32)],
        smem=1,
        args=(place, got),
    )


def project_body(place_ref, w_ref, *refs):
    ins, out_ref, rows = refs[:4], refs[4], refs[5]
    heads = w_ref.shape[0] // ins[0].shape[1]
    tokens = rows.shape[0] // heads
    for ref, step in zip(ins, STEPS):
        which = coset(place_ref[0] - step[0], place_ref[1] - step[1])
        for n in range(ref.shape[0] // 64):
            to = pl.multiple_of(64 * (SIDE * member_y(which, n) + n // 2), 64)
            rows[pl.ds(to, 64), :] = ref[64 * n : 64 * n + 64, :].astype(F32)
    left = [rows[pl.ds(h, tokens, stride=heads), :].astype(BF) for h in range(heads)]
    mixed = jnp.dot(jnp.concatenate(left, 1), w_ref[...], preferred_element_type=F32)
    out_ref[...] = mixed.astype(BF)


def project(place, weight, ins):
    deep, cols = weight.shape
    rows, width = ins[0].shape
    tokens = 4 * rows * width // deep
    return call(
        project_body,
        jax.ShapeDtypeStruct((tokens, cols), BF),
        flops=2 * tokens * deep * cols,
        scratch=[pltpu.VMEM((4 * rows, width), F32)],
        smem=1,
        args=(place, weight, *ins),
    )


def final_body(got_ref, out_ref):
    total = got_ref[0].astype(F32)
    for i in range(1, got_ref.shape[0]):
        total = total + got_ref[i].astype(F32)
    out_ref[...] = total.astype(BF)


def local(queries, cache_keys, cache_values, new_keys, new_values, cache_len, segment, out_weight):
    me = lax.axis_index("ctx").astype(jnp.int32)
    place = jnp.stack([me // SIDE, me % SIDE])
    block, heads, width = queries.shape
    seg = segment.reshape(-1, 128)
    near = prepare(
        cache_len,
        place,
        seg,
        cache_keys[:, 0, :],
        cache_values[:, 0, :],
        new_keys[:, 0, :],
        new_values[:, 0, :],
    )
    far = unpack(place, seg, shift(near[0][0], (0, 1)), shift(near[1][0], (0, -1)))
    mine = turn(near[0][2], share(queries.reshape(block * heads, width)))
    theirs = shift(mine, (1, 0))
    sums = attend(place, mine, near, (0, 0))
    their_sums = attend(place, theirs, near, (1, 0))
    their_part = attend_on(place, theirs, near, far, their_sums, (1, 0))
    part = attend_on(place, mine, near, far, sums, (0, 0))
    part = first_merge([part, shift(their_part, (-1, 0))])
    own = second_merge(place, exchange(part))
    mine = share(own)
    every = [mine] + [shift(mine, step) for step in STEPS[1:]]
    mixed = project(place, out_weight, every)
    mixed = mixed.reshape(lax.axis_size("kvh"), -1, mixed.shape[1])
    got = lax.all_to_all(mixed, "kvh", 0, 0, tiled=True)
    return call(final_body, jax.ShapeDtypeStruct(got.shape[1:], BF), args=(got,))


def solution(mesh):
    in_specs = (
        P("ctx", "kvh", None),
        P("ctx", "kvh", None),
        P("ctx", "kvh", None),
        P("ctx", "kvh", None),
        P("ctx", "kvh", None),
        P("ctx"),
        P(),
        P("kvh", "ctx"),
    )
    out_specs = P("kvh", "ctx")
    return jax.shard_map(local, mesh=mesh, in_specs=in_specs, out_specs=out_specs, check_vma=False)
```

```python
import functools

import jax
import jax.numpy as jnp
from jax import lax
from jax.experimental import pallas as pl
from jax.experimental.pallas import tpu as pltpu
from jax.sharding import PartitionSpec as P

BF = jnp.bfloat16
F32 = jnp.float32
LOG2E = 1.4426950408889634
LIMIT = 48 * 1024 * 1024
HUGE = 2.0**100
SIDE = 8
STEPS = ((0, 0), (1, 0), (-1, 0), (0, 1))
TAIL = 32


def shift(value, step):
    pairs = []
    for y in range(SIDE):
        for z in range(SIDE):
            to = ((y + step[0]) % SIDE) * SIDE + (z + step[1]) % SIDE
            pairs.append((y * SIDE + z, to))
    return lax.ppermute(value, "ctx", pairs)


def coset(y, z):
    return lax.rem(y + 2 * z + 4 * SIDE, 4)


def member_y(which, i):
    return lax.rem(which + 2 * (i // 2), 4) + 4 * (i % 2)


def cosets():
    return [
        [((v + 2 * z) % 4 + 4 * b) * SIDE + z for z in range(SIDE) for b in range(2)]
        for v in range(4)
    ]


def exchange(value):
    return lax.all_to_all(value, "ctx", 0, 0, axis_index_groups=cosets(), tiled=True)


def share(value):
    copies = jnp.broadcast_to(value[None], (16,) + value.shape)
    return exchange(copies).reshape(16 * value.shape[0], value.shape[1])


def call(body, out_shape, flops=0, moved=0, scratch=(), smem=0, args=()):
    vmem = pl.BlockSpec(memory_space=pltpu.VMEM)
    scalars = pl.BlockSpec(memory_space=pltpu.SMEM)
    specs = [scalars] * smem + [vmem] * (len(args) - smem)
    return pl.pallas_call(
        body,
        out_shape=out_shape,
        in_specs=specs,
        out_specs=jax.tree.map(lambda _: vmem, out_shape),
        scratch_shapes=list(scratch),
        compiler_params=pltpu.CompilerParams(vmem_limit_bytes=LIMIT),
        cost_estimate=pl.CostEstimate(flops=flops, bytes_accessed=moved, transcendentals=0),
    )(*args)


def turned(kv_ref, span, fresh, live, vt_ref):
    width = kv_ref.shape[1]
    slots = span - fresh
    step = 256
    for at in range(0, slots, step):
        vals = kv_ref[span + at : span + at + step, :].astype(F32)
        vt_ref[0:width, at : at + step] = vals.T.astype(BF)
        flags = lax.broadcasted_iota(jnp.int32, (16, step), 1) + at < live
        vt_ref[width:, at : at + step] = flags.astype(F32).astype(BF)
    if fresh:
        vals = kv_ref[span + slots : 2 * span, :].astype(F32)
        vals = jnp.concatenate([vals, jnp.zeros((128 - fresh, width), F32)], 0)
        vt_ref[0:width, slots:] = vals.T.astype(BF)
        flags = lax.broadcasted_iota(jnp.int32, (16, 128), 1) < 4
        vt_ref[width:, slots:] = flags.astype(F32).astype(BF)


def bounds_of(first, seg, live, b_ref):
    line = lax.broadcasted_iota(jnp.int32, (16, 128), 0)
    never = 1 << 30
    ends = jnp.full((16, 128), never, jnp.int32)
    seg = seg.astype(F32)
    spot = lax.broadcasted_iota(jnp.int32, seg.shape, 0) * 128 + lax.broadcasted_iota(
        jnp.int32, seg.shape, 1
    )

    def whole(part):
        return jnp.sum(jnp.sum(part, axis=0, keepdims=True), axis=1, keepdims=True)

    for j in range(4):
        own = whole(jnp.where(spot == first + j, seg, 0.0))
        count = whole(jnp.where(seg <= own, 1.0, 0.0))
        ends = jnp.where(line == j, count.astype(jnp.int32), ends)
    b_ref[0:16, :] = jnp.where(line < 4, line + first, never)
    b_ref[16:32, :] = ends
    b_ref[32:40, :] = jnp.zeros((8, 128), jnp.int32) + live


def prepare_body(live_ref, place_ref, seg_ref, k_ref, v_ref, fk_ref, fv_ref, *outs):
    live = live_ref[0]
    slots, width = k_ref.shape
    half = slots // 2
    step = 256
    first = k_ref[0:16, :].astype(F32)[0:1, :]
    line = lax.broadcasted_iota(jnp.int32, (16, width), 0)
    size = jnp.where(line == 0, live // 64, jnp.where(line == 1, lax.rem(live, 64), 0))
    pad = jnp.zeros((16 - fk_ref.shape[0], width), F32)
    for n in range(2):
        kv_ref, vt_ref, b_ref = outs[3 * n : 3 * n + 3]
        fresh = 16 * n
        span = half + fresh
        for at in range(0, half, step):
            rows = slice(n * half + at, n * half + at + step)
            alive = lax.broadcasted_iota(jnp.int32, (step, width), 0) + n * half + at < live
            keys = jnp.where(alive, k_ref[rows, :].astype(F32), first)
            kv_ref[at : at + step, :] = keys.astype(BF)
            vals = jnp.where(alive, v_ref[rows, :].astype(F32), 0.0)
            kv_ref[span + at : span + at + step, :] = vals.astype(BF)
        if fresh:
            for at, ref in ((half, fk_ref), (span + half, fv_ref)):
                new = jnp.concatenate([ref[...].astype(F32), pad], 0)
                kv_ref[at : at + 16, :] = new.astype(BF)
        kv_ref[2 * span :, :] = size.astype(F32).astype(BF)
        turned(kv_ref, span, fresh, live - n * half, vt_ref)
        first_token = 4 * (SIDE * place_ref[0] + place_ref[1])
        if fresh:
            bounds_of(first_token, seg_ref[...], live - n * half, b_ref)
        else:
            b_ref[...] = jnp.zeros(b_ref.shape, jnp.int32) + live


def ready_shapes(half, n, width):
    return [
        jax.ShapeDtypeStruct((width + 16, half + 128 * n), BF),
        jax.ShapeDtypeStruct((40, 128), jnp.int32),
    ]


def prepare(live, place, seg, keys, vals, fresh_k, fresh_v):
    slots, width = keys.shape
    half = slots // 2
    out = []
    for n in range(2):
        out.append(jax.ShapeDtypeStruct((2 * (half + 16 * n) + 16, width), BF))
        out += ready_shapes(half, n, width)
    args = (live, place, seg, keys, vals, fresh_k, fresh_v)
    got = call(prepare_body, out, smem=2, args=args)
    return tuple(got[:3]), tuple(got[3:])


def unpack_body(place_ref, seg_ref, lower_ref, upper_ref, one_ref, two_ref, *outs):
    for n, kv_ref in enumerate((lower_ref, upper_ref)):
        vt_ref, b_ref = outs[2 * n : 2 * n + 2]
        span = (kv_ref.shape[0] - 16) // 2
        fresh = 16 * n
        size = kv_ref[2 * span :, :].astype(F32)
        live = jnp.max(64.0 * size[0:1] + size[1:2]).astype(jnp.int32)
        live = live - n * (span - fresh)
        turned(kv_ref, span, fresh, live, vt_ref)
        from_z = lax.rem(place_ref[1] + 1, SIDE)
        if fresh:
            bounds_of(4 * (SIDE * place_ref[0] + from_z), seg_ref[...], live, b_ref)
        else:
            b_ref[...] = jnp.zeros(b_ref.shape, jnp.int32) + live


def unpack(place, seg, lower, upper, one, two):
    half, width = (lower.shape[0] - 16) // 2, lower.shape[1]
    out = ready_shapes(half, 0, width) + ready_shapes(half, 1, width)
    got = call(unpack_body, out, smem=1, args=(place, seg, lower, upper, one, two))
    return (lower, *got[:2]), (upper, *got[2:])


def turn_body(bound_ref, q_ref, out_ref):
    for at in range(0, q_ref.shape[0], 256):
        out_ref[:, at : at + 256] = q_ref[at : at + 256, :].astype(F32).T.astype(BF)


def turn(bounds, query):
    out = jax.ShapeDtypeStruct(query.shape[::-1], BF)
    return call(turn_body, out, args=(bounds, query))


def three(value):
    parts = []
    for _ in range(3):
        top = value.astype(BF).astype(F32)
        parts.append(top)
        value = value - top
    return parts


def attend_body(step, begin, place_ref, qt_ref, *refs):
    count = 2 if begin else 4
    shards = [refs[3 * n : 3 * n + 3] for n in range(count)]
    if begin:
        acc_out, peak_out = refs[6:]
    else:
        acc_in, peak_in, o_ref, lse_ref, worst_ref = refs[12:]
    width = qt_ref.shape[0]
    slots = shards[0][1].shape[1]
    rows = 256
    heads = 16
    pieces = qt_ref.shape[1] // rows
    factor = LOG2E / width**0.5
    lane = lax.broadcasted_iota(jnp.int32, (16, rows), 1)
    which = coset(place_ref[0] - step[0], place_ref[1] - step[1])

    def cuts_of(n):
        return [(n, at, 256) for at in range(0, slots, 256)] + [(n, slots, 16)] * (n % 2)

    def score(query, cut, i, exact=False):
        n, at, deep = cut
        kv_ref, vt_ref, b_ref = shards[n]
        part = jnp.dot(kv_ref[at : at + deep, :], query, preferred_element_type=F32)
        if deep == 16:
            opens = jnp.concatenate([b_ref[0:16, :]] * 2, 1)
            ends = jnp.concatenate([b_ref[16:32, :]] * 2, 1)
            member = 4 * i + lane // 64
            token = 32 * member_y(which, member) + 4 * (member // 2)
            token = token + lax.rem(lane // heads, 4)
            part = jnp.where((token >= opens) & (token < ends), part, -jnp.inf)
        elif exact:
            live = jnp.concatenate([b_ref[32:33, :]] * 2, 1)
            alive = lax.broadcasted_iota(jnp.int32, (deep, rows), 0) + at < live
            part = jnp.where(alive, part, -jnp.inf)
        return part

    def most(part):
        return jnp.max(part, axis=0, keepdims=True)

    def weigh(part, cut, peak, total):
        weight = jnp.exp2((part - peak) * factor).astype(BF)
        n, at, wide = cut
        if wide == 16:
            weight = jnp.concatenate([weight, jnp.zeros((112, rows), BF)], 0)
            wide = 128
        add = jnp.dot(shards[n][1][:, at : at + wide], weight, preferred_element_type=F32)
        return add if total is None else total + add

    def finish(i, peak, total):
        count = total[width : width + 1, :]
        out = total[0:width, :] * (1.0 / count)
        at = i * rows
        if not isinstance(i, int):
            at = pl.multiple_of(at, rows)
        o_ref[pl.ds(at, rows), :] = out.T.astype(BF)
        lse = peak * factor + jnp.log(count) * LOG2E
        lse_ref[i] = jnp.concatenate([lse[:, 0:128], lse[:, 128:256]], 0)
        return count

    def query_of(i):
        return qt_ref[:, i * rows : (i + 1) * rows]

    cuts = cuts_of(count - 2) + cuts_of(count - 1)
    worst = None
    todo = [(i, cut) for i in range(pieces) for cut in cuts]
    ahead = score(query_of(0), cuts[0], 0)
    peak_ahead = most(ahead)
    for at_todo, (i, cut) in enumerate(todo):
        part, at = ahead, slice(i * rows, (i + 1) * rows)
        if cut == cuts[0]:
            peak = peak_ahead if begin else peak_in[0:1, at]
            total = None if begin else acc_in[:, at]
        if at_todo + 1 < len(todo):
            j, later = todo[at_todo + 1]
            ahead = score(query_of(j), later, j)
            if begin and later == cuts[0]:
                peak_ahead = most(ahead)
        total = weigh(part, cut, peak, total)
        if cut == cuts[-1]:
            if begin:
                acc_out[:, at] = total
                peak_out[:, at] = jnp.broadcast_to(peak, (8, rows))
            else:
                counts = finish(i, peak, total)
                worst = counts if worst is None else jnp.maximum(worst, counts)
    if begin:
        return
    worst_ref[...] = jnp.broadcast_to(worst, worst_ref.shape)

    @pl.when(jnp.logical_not(jnp.max(worst_ref[0:1, :]) < HUGE))
    def _():
        def slow(i, carry):
            query = qt_ref[:, pl.ds(pl.multiple_of(i * rows, rows), rows)]
            peak, total = None, None
            every = sum((cuts_of(n) for n in range(count)), [])
            for cut in every:
                top = most(score(query, cut, i, True))
                peak = top if peak is None else jnp.maximum(peak, top)
            for cut in every:
                total = weigh(score(query, cut, i, True), cut, peak, total)
            finish(i, peak, total)
            return carry

        lax.fori_loop(0, pieces, slow, 0)

    lse = jnp.concatenate([lse_ref[i] for i in range(pieces)], 0)
    parts = three(lse) + [jnp.zeros((8, 128), F32)]
    o_ref[pieces * rows :, :] = jnp.concatenate(parts, 0).astype(BF)


def attend(place, query, near, step):
    width, rows = query.shape
    return call(
        functools.partial(attend_body, step, True),
        [
            jax.ShapeDtypeStruct((width + 16, rows), F32),
            jax.ShapeDtypeStruct((8, rows), F32),
        ],
        flops=8 * rows * near[0][1].shape[1] * 256,
        moved=8 * near[0][0].size,
        smem=1,
        args=(place, query, *near[0], *near[1]),
    )


def attend_on(place, query, near, far, sums, step):
    width, rows = query.shape
    return call(
        functools.partial(attend_body, step, False),
        jax.ShapeDtypeStruct((rows + TAIL, width), BF),
        flops=8 * rows * far[0][1].shape[1] * 256,
        moved=8 * far[0][0].size,
        scratch=[pltpu.VMEM((4, 2, 128), F32), pltpu.VMEM((8, 256), F32)],
        smem=1,
        args=(place, query, *near[0], *near[1], *far[0], *far[1], *sums),
    )


def diagonal(rows):
    return lax.broadcasted_iota(jnp.int32, (rows, 128), 0) == lax.broadcasted_iota(
        jnp.int32, (rows, 128), 1
    )


def spread(row, eye):
    return jnp.sum(jnp.where(eye, row, 0.0), axis=1, keepdims=True)


def first_body(*refs):
    ins, out_ref = refs[:-1], refs[-1]
    rows = ins[0].shape[0] - TAIL
    eye = diagonal(128)
    logs = []
    for ref in ins:
        tail = ref[rows:, :].astype(F32)
        logs.append(tail[0:8] + tail[8:16] + tail[16:24])
    top = functools.reduce(jnp.maximum, logs)
    weights = [jnp.exp2(log - top) for log in logs]
    total = functools.reduce(jnp.add, weights)
    lse = top + jnp.log(total) * LOG2E
    weights = [w / total for w in weights]
    parts = []
    for _ in range(3):
        high = lse.astype(BF).astype(F32)
        parts.append(high)
        lse = lse - high
    empty = jnp.zeros((5, 128), F32)
    for b in range(rows // 128):
        merged = None
        for ref, weight in zip(ins, weights):
            term = ref[b * 128 : (b + 1) * 128, :].astype(F32) * spread(weight[b : b + 1], eye)
            merged = term if merged is None else merged + term
        merged = merged.astype(BF)
        tail = jnp.concatenate([p[b : b + 1] for p in parts] + [empty], 0).astype(BF)
        for j in range(2):
            out_ref[2 * b + j, 0:64, :] = merged[64 * j : 64 * j + 64, :]
            out_ref[2 * b + j, 64:72, :] = tail


def first_merge(ins):
    rows, width = ins[0].shape
    out = jax.ShapeDtypeStruct(((rows - TAIL) // 64, 72, width), BF)
    return call(first_body, out, args=tuple(ins))


def second_body(place_ref, got_ref, out_ref, logs):
    parts = got_ref.shape[0]
    for c in range(parts):
        tail = got_ref[c, 64:72, :].astype(F32)
        logs[c : c + 1, :] = tail[0:1] + tail[1:2] + tail[2:3]
    lse = logs[...]
    lse = jnp.where(place_ref[0] // 4 == 1, pltpu.roll(lse, 64, 1), lse)
    weight = jnp.exp2(lse - jnp.max(lse, axis=0, keepdims=True))
    weight = weight / jnp.sum(weight, axis=0, keepdims=True)
    eye = diagonal(64)
    total = None
    for c in range(parts):
        term = got_ref[c, 0:64, :].astype(F32) * spread(weight[c : c + 1, :], eye)
        total = term if total is None else total + term
    out_ref[...] = total.astype(BF)


def second_merge(place, got):
    return call(
        second_body,
        jax.ShapeDtypeStruct((64, got.shape[2]), BF),
        scratch=[pltpu.VMEM((got.shape[0], 128), F32)],
        smem=1,
        args=(place, got),
    )


def project_body(place_ref, w_ref, *refs):
    ins, out_ref, rows = refs[:4], refs[4], refs[5]
    heads = w_ref.shape[0] // ins[0].shape[1]
    tokens = rows.shape[0] // heads
    for ref, step in zip(ins, STEPS):
        which = coset(place_ref[0] - step[0], place_ref[1] - step[1])
        for n in range(ref.shape[0] // 64):
            to = pl.multiple_of(64 * (SIDE * member_y(which, n) + n // 2), 64)
            rows[pl.ds(to, 64), :] = ref[64 * n : 64 * n + 64, :].astype(F32)
    left = [rows[pl.ds(h, tokens, stride=heads), :].astype(BF) for h in range(heads)]
    mixed = jnp.dot(jnp.concatenate(left, 1), w_ref[...], preferred_element_type=F32)
    out_ref[...] = mixed.astype(BF)


def project(place, weight, ins):
    deep, cols = weight.shape
    rows, width = ins[0].shape
    tokens = 4 * rows * width // deep
    return call(
        project_body,
        jax.ShapeDtypeStruct((tokens, cols), BF),
        flops=2 * tokens * deep * cols,
        scratch=[pltpu.VMEM((4 * rows, width), F32)],
        smem=1,
        args=(place, weight, *ins),
    )


def final_body(got_ref, out_ref):
    total = got_ref[0].astype(F32)
    for i in range(1, got_ref.shape[0]):
        total = total + got_ref[i].astype(F32)
    out_ref[...] = total.astype(BF)


def local(queries, cache_keys, cache_values, new_keys, new_values, cache_len, segment, out_weight):
    me = lax.axis_index("ctx").astype(jnp.int32)
    place = jnp.stack([me // SIDE, me % SIDE])
    block, heads, width = queries.shape
    seg = segment.reshape(-1, 128)
    near = prepare(
        cache_len,
        place,
        seg,
        cache_keys[:, 0, :],
        cache_values[:, 0, :],
        new_keys[:, 0, :],
        new_values[:, 0, :],
    )
    lower, upper = shift(near[0][0], (0, 1)), shift(near[1][0], (0, -1))
    mine = turn(near[0][2], share(queries.reshape(block * heads, width)))
    theirs = shift(mine, (1, 0))
    sums = attend(place, mine, near, (0, 0))
    their_sums = attend(place, theirs, near, (1, 0))
    far = unpack(place, seg, lower, upper, sums[1], their_sums[1])
    their_part = attend_on(place, theirs, near, far, their_sums, (1, 0))
    part = attend_on(place, mine, near, far, sums, (0, 0))
    part = first_merge([part, shift(their_part, (-1, 0))])
    own = second_merge(place, exchange(part))
    mine = share(own)
    every = [mine] + [shift(mine, step) for step in STEPS[1:]]
    mixed = project(place, out_weight, every)
    mixed = mixed.reshape(lax.axis_size("kvh"), -1, mixed.shape[1])
    got = lax.all_to_all(mixed, "kvh", 0, 0, tiled=True)
    return call(final_body, jax.ShapeDtypeStruct(got.shape[1:], BF), args=(got,))


def solution(mesh):
    in_specs = (
        P("ctx", "kvh", None),
        P("ctx", "kvh", None),
        P("ctx", "kvh", None),
        P("ctx", "kvh", None),
        P("ctx", "kvh", None),
        P("ctx"),
        P(),
        P("kvh", "ctx"),
    )
    out_specs = P("kvh", "ctx")
    return jax.shard_map(local, mesh=mesh, in_specs=in_specs, out_specs=out_specs, check_vma=False)
```

```python
import functools

import jax
import jax.numpy as jnp
from jax import lax
from jax.experimental import pallas as pl
from jax.experimental.pallas import tpu as pltpu
from jax.sharding import PartitionSpec as P

BF = jnp.bfloat16
F32 = jnp.float32
LOG2E = 1.4426950408889634
LIMIT = 48 * 1024 * 1024
HUGE = 2.0**100
SIDE = 8
STEPS = ((0, 0), (1, 0), (-1, 0), (0, 1))
TAIL = 32


def shift(value, step):
    pairs = []
    for y in range(SIDE):
        for z in range(SIDE):
            to = ((y + step[0]) % SIDE) * SIDE + (z + step[1]) % SIDE
            pairs.append((y * SIDE + z, to))
    return lax.ppermute(value, "ctx", pairs)


def row_of(place_ref):
    return lax.shift_right_logical(place_ref[0], 3)


def column_of(place_ref):
    return lax.bitwise_and(place_ref[0], SIDE - 1)


def coset(y, z):
    return lax.rem(y + 2 * z + 4 * SIDE, 4)


def member_y(which, i):
    return lax.rem(which + 2 * (i // 2), 4) + 4 * (i % 2)


def cosets():
    return [
        [((v + 2 * z) % 4 + 4 * b) * SIDE + z for z in range(SIDE) for b in range(2)]
        for v in range(4)
    ]


def exchange(value):
    return lax.all_to_all(value, "ctx", 0, 0, axis_index_groups=cosets(), tiled=True)


def share(value):
    copies = jnp.broadcast_to(value[None], (16,) + value.shape)
    return exchange(copies).reshape(16 * value.shape[0], value.shape[1])


def call(body, out_shape, flops=0, moved=0, scratch=(), smem=0, args=()):
    vmem = pl.BlockSpec(memory_space=pltpu.VMEM)
    scalars = pl.BlockSpec(memory_space=pltpu.SMEM)
    specs = [scalars] * smem + [vmem] * (len(args) - smem)
    return pl.pallas_call(
        body,
        out_shape=out_shape,
        in_specs=specs,
        out_specs=jax.tree.map(lambda _: vmem, out_shape),
        scratch_shapes=list(scratch),
        compiler_params=pltpu.CompilerParams(vmem_limit_bytes=LIMIT),
        cost_estimate=pl.CostEstimate(flops=flops, bytes_accessed=moved, transcendentals=0),
    )(*args)


def turned(kv_ref, span, fresh, live, vt_ref):
    width = kv_ref.shape[1]
    slots = span - fresh
    step = 256
    for at in range(0, slots, step):
        vals = kv_ref[span + at : span + at + step, :].astype(F32)
        vt_ref[0:width, at : at + step] = vals.T.astype(BF)
        flags = lax.broadcasted_iota(jnp.int32, (16, step), 1) + at < live
        vt_ref[width:, at : at + step] = flags.astype(F32).astype(BF)
    if fresh:
        vals = kv_ref[span + slots : 2 * span, :].astype(F32)
        vals = jnp.concatenate([vals, jnp.zeros((128 - fresh, width), F32)], 0)
        vt_ref[0:width, slots:] = vals.T.astype(BF)
        flags = lax.broadcasted_iota(jnp.int32, (16, 128), 1) < 4
        vt_ref[width:, slots:] = flags.astype(F32).astype(BF)


def bounds_of(first, seg, live, b_ref):
    line = lax.broadcasted_iota(jnp.int32, (16, 128), 0)
    never = 1 << 30
    ends = jnp.full((16, 128), never, jnp.int32)
    seg = seg.astype(F32)
    spot = lax.broadcasted_iota(jnp.int32, seg.shape, 0) * 128 + lax.broadcasted_iota(
        jnp.int32, seg.shape, 1
    )

    def whole(part):
        return jnp.sum(jnp.sum(part, axis=0, keepdims=True), axis=1, keepdims=True)

    for j in range(4):
        own = whole(jnp.where(spot == first + j, seg, 0.0))
        count = whole(jnp.where(seg <= own, 1.0, 0.0))
        ends = jnp.where(line == j, count.astype(jnp.int32), ends)
    b_ref[0:16, :] = jnp.where(line < 4, line + first, never)
    b_ref[16:32, :] = ends
    b_ref[32:40, :] = jnp.zeros((8, 128), jnp.int32) + live


def prepare_body(live_ref, place_ref, seg_ref, k_ref, v_ref, fk_ref, fv_ref, *outs):
    live = live_ref[0]
    slots, width = k_ref.shape
    half = slots // 2
    step = 256
    first = k_ref[0:16, :].astype(F32)[0:1, :]
    line = lax.broadcasted_iota(jnp.int32, (16, width), 0)
    size = jnp.where(line == 0, live // 64, jnp.where(line == 1, lax.rem(live, 64), 0))
    pad = jnp.zeros((16 - fk_ref.shape[0], width), F32)
    for n in range(2):
        kv_ref, vt_ref, b_ref = outs[3 * n : 3 * n + 3]
        fresh = 16 * n
        span = half + fresh
        for at in range(0, half, step):
            rows = slice(n * half + at, n * half + at + step)
            alive = lax.broadcasted_iota(jnp.int32, (step, width), 0) + n * half + at < live
            keys = jnp.where(alive, k_ref[rows, :].astype(F32), first)
            kv_ref[at : at + step, :] = keys.astype(BF)
            vals = jnp.where(alive, v_ref[rows, :].astype(F32), 0.0)
            kv_ref[span + at : span + at + step, :] = vals.astype(BF)
        if fresh:
            for at, ref in ((half, fk_ref), (span + half, fv_ref)):
                new = jnp.concatenate([ref[...].astype(F32), pad], 0)
                kv_ref[at : at + 16, :] = new.astype(BF)
        kv_ref[2 * span :, :] = size.astype(F32).astype(BF)
        turned(kv_ref, span, fresh, live - n * half, vt_ref)
        first_token = 4 * (SIDE * row_of(place_ref) + column_of(place_ref))
        if fresh:
            bounds_of(first_token, seg_ref[...], live - n * half, b_ref)
        else:
            b_ref[...] = jnp.zeros(b_ref.shape, jnp.int32) + live


def ready_shapes(half, n, width):
    return [
        jax.ShapeDtypeStruct((width + 16, half + 128 * n), BF),
        jax.ShapeDtypeStruct((40, 128), jnp.int32),
    ]


def prepare(live, place, seg, keys, vals, fresh_k, fresh_v):
    slots, width = keys.shape
    half = slots // 2
    out = []
    for n in range(2):
        out.append(jax.ShapeDtypeStruct((2 * (half + 16 * n) + 16, width), BF))
        out += ready_shapes(half, n, width)
    args = (live, place, seg, keys, vals, fresh_k, fresh_v)
    got = call(prepare_body, out, smem=2, args=args)
    return tuple(got[:3]), tuple(got[3:])


def unpack_body(place_ref, seg_ref, lower_ref, upper_ref, one_ref, two_ref, *outs):
    for n, kv_ref in enumerate((lower_ref, upper_ref)):
        vt_ref, b_ref = outs[2 * n : 2 * n + 2]
        span = (kv_ref.shape[0] - 16) // 2
        fresh = 16 * n
        size = kv_ref[2 * span :, :].astype(F32)
        live = jnp.max(64.0 * size[0:1] + size[1:2]).astype(jnp.int32)
        live = live - n * (span - fresh)
        turned(kv_ref, span, fresh, live, vt_ref)
        from_z = lax.rem(column_of(place_ref) + 1, SIDE)
        if fresh:
            bounds_of(4 * (SIDE * row_of(place_ref) + from_z), seg_ref[...], live, b_ref)
        else:
            b_ref[...] = jnp.zeros(b_ref.shape, jnp.int32) + live


def unpack(place, seg, lower, upper, one, two):
    half, width = (lower.shape[0] - 16) // 2, lower.shape[1]
    out = ready_shapes(half, 0, width) + ready_shapes(half, 1, width)
    got = call(unpack_body, out, smem=1, args=(place, seg, lower, upper, one, two))
    return (lower, *got[:2]), (upper, *got[2:])


def turn_body(bound_ref, q_ref, out_ref):
    for at in range(0, q_ref.shape[0], 256):
        out_ref[:, at : at + 256] = q_ref[at : at + 256, :].astype(F32).T.astype(BF)


def turn(bounds, query):
    out = jax.ShapeDtypeStruct(query.shape[::-1], BF)
    return call(turn_body, out, args=(bounds, query))


def three(value):
    parts = []
    for _ in range(3):
        top = value.astype(BF).astype(F32)
        parts.append(top)
        value = value - top
    return parts


def attend_body(step, begin, place_ref, qt_ref, *refs):
    count = 2 if begin else 4
    shards = [refs[3 * n : 3 * n + 3] for n in range(count)]
    if begin:
        acc_out, peak_out = refs[6:]
    else:
        acc_in, peak_in, o_ref, lse_ref, worst_ref = refs[12:]
    width = qt_ref.shape[0]
    slots = shards[0][1].shape[1]
    rows = 256
    heads = 16
    pieces = qt_ref.shape[1] // rows
    factor = LOG2E / width**0.5
    lane = lax.broadcasted_iota(jnp.int32, (16, rows), 1)
    which = coset(row_of(place_ref) - step[0], column_of(place_ref) - step[1])

    def cuts_of(n):
        return [(n, at, 256) for at in range(0, slots, 256)] + [(n, slots, 16)] * (n % 2)

    def score(query, cut, i, exact=False):
        n, at, deep = cut
        kv_ref, vt_ref, b_ref = shards[n]
        part = jnp.dot(kv_ref[at : at + deep, :], query, preferred_element_type=F32)
        if deep == 16:
            opens = jnp.concatenate([b_ref[0:16, :]] * 2, 1)
            ends = jnp.concatenate([b_ref[16:32, :]] * 2, 1)
            member = 4 * i + lane // 64
            token = 32 * member_y(which, member) + 4 * (member // 2)
            token = token + lax.rem(lane // heads, 4)
            part = jnp.where((token >= opens) & (token < ends), part, -jnp.inf)
        elif exact:
            live = jnp.concatenate([b_ref[32:33, :]] * 2, 1)
            alive = lax.broadcasted_iota(jnp.int32, (deep, rows), 0) + at < live
            part = jnp.where(alive, part, -jnp.inf)
        return part

    def most(part):
        return jnp.max(part, axis=0, keepdims=True)

    def weigh(part, cut, peak, total):
        weight = jnp.exp2((part - peak) * factor).astype(BF)
        n, at, wide = cut
        if wide == 16:
            weight = jnp.concatenate([weight, jnp.zeros((112, rows), BF)], 0)
            wide = 128
        add = jnp.dot(shards[n][1][:, at : at + wide], weight, preferred_element_type=F32)
        return add if total is None else total + add

    def finish(i, peak, total):
        count = total[width : width + 1, :]
        out = total[0:width, :] * (1.0 / count)
        at = i * rows
        if not isinstance(i, int):
            at = pl.multiple_of(at, rows)
        o_ref[pl.ds(at, rows), :] = out.T.astype(BF)
        lse = peak * factor + jnp.log(count) * LOG2E
        lse_ref[i] = jnp.concatenate([lse[:, 0:128], lse[:, 128:256]], 0)
        return count

    def query_of(i):
        return qt_ref[:, i * rows : (i + 1) * rows]

    cuts = cuts_of(count - 2) + cuts_of(count - 1)
    worst = None
    todo = [(i, cut) for i in range(pieces) for cut in cuts]
    ahead = score(query_of(0), cuts[0], 0)
    peak_ahead = most(ahead)
    for at_todo, (i, cut) in enumerate(todo):
        part, at = ahead, slice(i * rows, (i + 1) * rows)
        if cut == cuts[0]:
            peak = peak_ahead if begin else peak_in[0:1, at]
            total = None if begin else acc_in[:, at]
        if at_todo + 1 < len(todo):
            j, later = todo[at_todo + 1]
            ahead = score(query_of(j), later, j)
            if begin and later == cuts[0]:
                peak_ahead = most(ahead)
        total = weigh(part, cut, peak, total)
        if cut == cuts[-1]:
            if begin:
                acc_out[:, at] = total
                peak_out[:, at] = jnp.broadcast_to(peak, (8, rows))
            else:
                counts = finish(i, peak, total)
                worst = counts if worst is None else jnp.maximum(worst, counts)
    if begin:
        return
    worst_ref[...] = jnp.broadcast_to(worst, worst_ref.shape)

    @pl.when(jnp.logical_not(jnp.max(worst_ref[0:1, :]) < HUGE))
    def _():
        def slow(i, carry):
            query = qt_ref[:, pl.ds(pl.multiple_of(i * rows, rows), rows)]
            peak, total = None, None
            every = sum((cuts_of(n) for n in range(count)), [])
            for cut in every:
                top = most(score(query, cut, i, True))
                peak = top if peak is None else jnp.maximum(peak, top)
            for cut in every:
                total = weigh(score(query, cut, i, True), cut, peak, total)
            finish(i, peak, total)
            return carry

        lax.fori_loop(0, pieces, slow, 0)

    lse = jnp.concatenate([lse_ref[i] for i in range(pieces)], 0)
    parts = three(lse) + [jnp.zeros((8, 128), F32)]
    o_ref[pieces * rows :, :] = jnp.concatenate(parts, 0).astype(BF)


def attend(place, query, near, step):
    width, rows = query.shape
    return call(
        functools.partial(attend_body, step, True),
        [
            jax.ShapeDtypeStruct((width + 16, rows), F32),
            jax.ShapeDtypeStruct((8, rows), F32),
        ],
        flops=8 * rows * near[0][1].shape[1] * 256,
        moved=8 * near[0][0].size,
        smem=1,
        args=(place, query, *near[0], *near[1]),
    )


def attend_on(place, query, near, far, sums, step):
    width, rows = query.shape
    return call(
        functools.partial(attend_body, step, False),
        jax.ShapeDtypeStruct((rows + TAIL, width), BF),
        flops=8 * rows * far[0][1].shape[1] * 256,
        moved=8 * far[0][0].size,
        scratch=[pltpu.VMEM((4, 2, 128), F32), pltpu.VMEM((8, 256), F32)],
        smem=1,
        args=(place, query, *near[0], *near[1], *far[0], *far[1], *sums),
    )


def diagonal(rows):
    return lax.broadcasted_iota(jnp.int32, (rows, 128), 0) == lax.broadcasted_iota(
        jnp.int32, (rows, 128), 1
    )


def spread(row, eye):
    return jnp.sum(jnp.where(eye, row, 0.0), axis=1, keepdims=True)


def first_body(*refs):
    ins, out_ref = refs[:-1], refs[-1]
    rows = ins[0].shape[0] - TAIL
    eye = diagonal(128)
    logs = []
    for ref in ins:
        tail = ref[rows:, :].astype(F32)
        logs.append(tail[0:8] + tail[8:16] + tail[16:24])
    top = functools.reduce(jnp.maximum, logs)
    weights = [jnp.exp2(log - top) for log in logs]
    total = functools.reduce(jnp.add, weights)
    lse = top + jnp.log(total) * LOG2E
    weights = [w / total for w in weights]
    parts = []
    for _ in range(3):
        high = lse.astype(BF).astype(F32)
        parts.append(high)
        lse = lse - high
    empty = jnp.zeros((5, 128), F32)
    for b in range(rows // 128):
        merged = None
        for ref, weight in zip(ins, weights):
            term = ref[b * 128 : (b + 1) * 128, :].astype(F32) * spread(weight[b : b + 1], eye)
            merged = term if merged is None else merged + term
        merged = merged.astype(BF)
        tail = jnp.concatenate([p[b : b + 1] for p in parts] + [empty], 0).astype(BF)
        for j in range(2):
            out_ref[2 * b + j, 0:64, :] = merged[64 * j : 64 * j + 64, :]
            out_ref[2 * b + j, 64:72, :] = tail


def first_merge(ins):
    rows, width = ins[0].shape
    out = jax.ShapeDtypeStruct(((rows - TAIL) // 64, 72, width), BF)
    return call(first_body, out, args=tuple(ins))


def second_body(place_ref, got_ref, out_ref, logs):
    parts = got_ref.shape[0]
    for c in range(parts):
        tail = got_ref[c, 64:72, :].astype(F32)
        logs[c : c + 1, :] = tail[0:1] + tail[1:2] + tail[2:3]
    lse = logs[...]
    lse = jnp.where(row_of(place_ref) // 4 == 1, pltpu.roll(lse, 64, 1), lse)
    weight = jnp.exp2(lse - jnp.max(lse, axis=0, keepdims=True))
    weight = weight / jnp.sum(weight, axis=0, keepdims=True)
    lane = lax.broadcasted_iota(jnp.int32, (64, 128), 1)
    eye = lax.bitwise_and(lane, 63) == lax.broadcasted_iota(jnp.int32, (64, 128), 0)
    moved = pltpu.roll(weight, 64, 1)
    high, low = [], []
    for c in range(0, parts, 2):
        pair = jnp.where(lane[0:1] < 64, weight[c : c + 1], moved[c + 1 : c + 2])
        pair = jnp.where(eye, pair, 0.0)
        high.append(pair.astype(BF))
        low.append((pair - high[-1].astype(F32)).astype(BF))
    rows = jnp.concatenate([got_ref[c, 0:64, :] for c in range(parts)], 0)
    total = jnp.dot(jnp.concatenate(high, 1), rows, preferred_element_type=F32)
    total = total + jnp.dot(jnp.concatenate(low, 1), rows, preferred_element_type=F32)
    out_ref[...] = total.astype(BF)


def second_merge(place, got):
    return call(
        second_body,
        jax.ShapeDtypeStruct((64, got.shape[2]), BF),
        scratch=[pltpu.VMEM((got.shape[0], 128), F32)],
        smem=1,
        args=(place, got),
    )


def project_body(place_ref, w_ref, *refs):
    ins, out_ref, rows = refs[:4], refs[4], refs[5]
    heads = w_ref.shape[0] // ins[0].shape[1]
    tokens = rows.shape[0] // heads
    for ref, step in zip(ins, STEPS):
        which = coset(row_of(place_ref) - step[0], column_of(place_ref) - step[1])
        for n in range(ref.shape[0] // 64):
            to = pl.multiple_of(64 * (SIDE * member_y(which, n) + n // 2), 64)
            rows[pl.ds(to, 64), :] = ref[64 * n : 64 * n + 64, :].astype(F32)
    left = [rows[pl.ds(h, tokens, stride=heads), :].astype(BF) for h in range(heads)]
    mixed = jnp.dot(jnp.concatenate(left, 1), w_ref[...], preferred_element_type=F32)
    out_ref[...] = mixed.astype(BF)


def project(place, weight, ins):
    deep, cols = weight.shape
    rows, width = ins[0].shape
    tokens = 4 * rows * width // deep
    return call(
        project_body,
        jax.ShapeDtypeStruct((tokens, cols), BF),
        flops=2 * tokens * deep * cols,
        scratch=[pltpu.VMEM((4 * rows, width), F32)],
        smem=1,
        args=(place, weight, *ins),
    )


def final_body(got_ref, out_ref):
    total = got_ref[0].astype(F32)
    for i in range(1, got_ref.shape[0]):
        total = total + got_ref[i].astype(F32)
    out_ref[...] = total.astype(BF)


def local(queries, cache_keys, cache_values, new_keys, new_values, cache_len, segment, out_weight):
    place = lax.axis_index("ctx").astype(jnp.int32).reshape(1)
    block, heads, width = queries.shape
    seg = segment.reshape(-1, 128)
    near = prepare(
        cache_len,
        place,
        seg,
        cache_keys[:, 0, :],
        cache_values[:, 0, :],
        new_keys[:, 0, :],
        new_values[:, 0, :],
    )
    lower, upper = shift(near[0][0], (0, 1)), shift(near[1][0], (0, -1))
    mine = turn(near[0][2], share(queries.reshape(block * heads, width)))
    theirs = shift(mine, (1, 0))
    sums = attend(place, mine, near, (0, 0))
    their_sums = attend(place, theirs, near, (1, 0))
    far = unpack(place, seg, lower, upper, sums[1], their_sums[1])
    their_part = attend_on(place, theirs, near, far, their_sums, (1, 0))
    part = attend_on(place, mine, near, far, sums, (0, 0))
    part = first_merge([part, shift(their_part, (-1, 0))])
    own = second_merge(place, exchange(part))
    mine = share(own)
    every = [mine] + [shift(mine, step) for step in STEPS[1:]]
    mixed = project(place, out_weight, every)
    mixed = mixed.reshape(lax.axis_size("kvh"), -1, mixed.shape[1])
    got = lax.all_to_all(mixed, "kvh", 0, 0, tiled=True)
    return call(final_body, jax.ShapeDtypeStruct(got.shape[1:], BF), args=(got,))


def solution(mesh):
    in_specs = (
        P("ctx", "kvh", None),
        P("ctx", "kvh", None),
        P("ctx", "kvh", None),
        P("ctx", "kvh", None),
        P("ctx", "kvh", None),
        P("ctx"),
        P(),
        P("kvh", "ctx"),
    )
    out_specs = P("kvh", "ctx")
    return jax.shard_map(local, mesh=mesh, in_specs=in_specs, out_specs=out_specs, check_vma=False)
```

```python
import functools

import jax
import jax.numpy as jnp
from jax import lax
from jax.experimental import pallas as pl
from jax.experimental.pallas import tpu as pltpu
from jax.sharding import PartitionSpec as P

BF = jnp.bfloat16
F32 = jnp.float32
LOG2E = 1.4426950408889634
LIMIT = 48 * 1024 * 1024
HUGE = 2.0**100
SIDE = 8
STEPS = ((0, 0), (1, 0), (-1, 0), (0, 1))
TAIL = 32


def shift(value, step):
    pairs = []
    for y in range(SIDE):
        for z in range(SIDE):
            to = ((y + step[0]) % SIDE) * SIDE + (z + step[1]) % SIDE
            pairs.append((y * SIDE + z, to))
    return lax.ppermute(value, "ctx", pairs)


def row_of(place_ref):
    return lax.shift_right_logical(place_ref[0], 3)


def column_of(place_ref):
    return lax.bitwise_and(place_ref[0], SIDE - 1)


def coset(y, z):
    return (y + 2 * z + 4 * SIDE) & 3


def member_y(which, i):
    return ((which + 2 * (i >> 1)) & 3) + 4 * (i & 1)


def cosets():
    return [
        [((v + 2 * z) % 4 + 4 * b) * SIDE + z for z in range(SIDE) for b in range(2)]
        for v in range(4)
    ]


def exchange(value):
    return lax.all_to_all(value, "ctx", 0, 0, axis_index_groups=cosets(), tiled=True)


def share(value):
    copies = jnp.broadcast_to(value[None], (16,) + value.shape)
    return exchange(copies).reshape(16 * value.shape[0], value.shape[1])


def call(body, out_shape, flops=0, moved=0, scratch=(), smem=0, args=()):
    vmem = pl.BlockSpec(memory_space=pltpu.VMEM)
    scalars = pl.BlockSpec(memory_space=pltpu.SMEM)
    specs = [scalars] * smem + [vmem] * (len(args) - smem)
    return pl.pallas_call(
        body,
        out_shape=out_shape,
        in_specs=specs,
        out_specs=jax.tree.map(lambda _: vmem, out_shape),
        scratch_shapes=list(scratch),
        compiler_params=pltpu.CompilerParams(vmem_limit_bytes=LIMIT),
        cost_estimate=pl.CostEstimate(flops=flops, bytes_accessed=moved, transcendentals=0),
    )(*args)


def turned(kv_ref, span, fresh, live, vt_ref):
    width = kv_ref.shape[1]
    slots = span - fresh
    step = 256
    for at in range(0, slots, step):
        vals = kv_ref[span + at : span + at + step, :].astype(F32)
        vt_ref[0:width, at : at + step] = vals.T.astype(BF)
        flags = lax.broadcasted_iota(jnp.int32, (16, step), 1) + at < live
        vt_ref[width:, at : at + step] = flags.astype(F32).astype(BF)
    if fresh:
        vals = kv_ref[span + slots : 2 * span, :].astype(F32)
        vals = jnp.concatenate([vals, jnp.zeros((128 - fresh, width), F32)], 0)
        vt_ref[0:width, slots:] = vals.T.astype(BF)
        flags = lax.broadcasted_iota(jnp.int32, (16, 128), 1) < 4
        vt_ref[width:, slots:] = flags.astype(F32).astype(BF)


def bounds_of(first, seg, live, b_ref):
    line = lax.broadcasted_iota(jnp.int32, (16, 128), 0)
    never = 1 << 30
    ends = jnp.full((16, 128), never, jnp.int32)
    seg = seg.astype(F32)
    spot = lax.broadcasted_iota(jnp.int32, seg.shape, 0) * 128 + lax.broadcasted_iota(
        jnp.int32, seg.shape, 1
    )

    def whole(part):
        return jnp.sum(jnp.sum(part, axis=0, keepdims=True), axis=1, keepdims=True)

    for j in range(4):
        own = whole(jnp.where(spot == first + j, seg, 0.0))
        count = whole(jnp.where(seg <= own, 1.0, 0.0))
        ends = jnp.where(line == j, count.astype(jnp.int32), ends)
    b_ref[0:16, :] = jnp.where(line < 4, line + first, never)
    b_ref[16:32, :] = ends
    b_ref[32:40, :] = jnp.zeros((8, 128), jnp.int32) + live


def prepare_body(live_ref, place_ref, seg_ref, k_ref, v_ref, fk_ref, fv_ref, *outs):
    live = live_ref[0]
    slots, width = k_ref.shape
    half = slots // 2
    step = 256
    first = k_ref[0:16, :].astype(F32)[0:1, :]
    line = lax.broadcasted_iota(jnp.int32, (16, width), 0)
    size = jnp.where(line == 0, live >> 6, jnp.where(line == 1, live & 63, 0))
    pad = jnp.zeros((16 - fk_ref.shape[0], width), F32)
    for n in range(2):
        kv_ref, vt_ref, b_ref = outs[3 * n : 3 * n + 3]
        fresh = 16 * n
        span = half + fresh
        for at in range(0, half, step):
            rows = slice(n * half + at, n * half + at + step)
            alive = lax.broadcasted_iota(jnp.int32, (step, width), 0) + n * half + at < live
            keys = jnp.where(alive, k_ref[rows, :].astype(F32), first)
            kv_ref[at : at + step, :] = keys.astype(BF)
            vals = jnp.where(alive, v_ref[rows, :].astype(F32), 0.0)
            kv_ref[span + at : span + at + step, :] = vals.astype(BF)
        if fresh:
            for at, ref in ((half, fk_ref), (span + half, fv_ref)):
                new = jnp.concatenate([ref[...].astype(F32), pad], 0)
                kv_ref[at : at + 16, :] = new.astype(BF)
        kv_ref[2 * span :, :] = size.astype(F32).astype(BF)
        turned(kv_ref, span, fresh, live - n * half, vt_ref)
        first_token = 4 * (SIDE * row_of(place_ref) + column_of(place_ref))
        if fresh:
            bounds_of(first_token, seg_ref[...], live - n * half, b_ref)
        else:
            b_ref[...] = jnp.zeros(b_ref.shape, jnp.int32) + live


def ready_shapes(half, n, width):
    return [
        jax.ShapeDtypeStruct((width + 16, half + 128 * n), BF),
        jax.ShapeDtypeStruct((40, 128), jnp.int32),
    ]


def prepare(live, place, seg, keys, vals, fresh_k, fresh_v):
    slots, width = keys.shape
    half = slots // 2
    out = []
    for n in range(2):
        out.append(jax.ShapeDtypeStruct((2 * (half + 16 * n) + 16, width), BF))
        out += ready_shapes(half, n, width)
    args = (live, place, seg, keys, vals, fresh_k, fresh_v)
    got = call(prepare_body, out, smem=2, args=args)
    return tuple(got[:3]), tuple(got[3:])


def unpack_body(place_ref, seg_ref, lower_ref, upper_ref, one_ref, two_ref, *outs):
    for n, kv_ref in enumerate((lower_ref, upper_ref)):
        vt_ref, b_ref = outs[2 * n : 2 * n + 2]
        span = (kv_ref.shape[0] - 16) // 2
        fresh = 16 * n
        size = kv_ref[2 * span :, :].astype(F32)
        live = jnp.max(64.0 * size[0:1] + size[1:2]).astype(jnp.int32)
        live = live - n * (span - fresh)
        turned(kv_ref, span, fresh, live, vt_ref)
        from_z = (column_of(place_ref) + 1) & (SIDE - 1)
        if fresh:
            bounds_of(4 * (SIDE * row_of(place_ref) + from_z), seg_ref[...], live, b_ref)
        else:
            b_ref[...] = jnp.zeros(b_ref.shape, jnp.int32) + live


def unpack(place, seg, lower, upper, one, two):
    half, width = (lower.shape[0] - 16) // 2, lower.shape[1]
    out = ready_shapes(half, 0, width) + ready_shapes(half, 1, width)
    got = call(unpack_body, out, smem=1, args=(place, seg, lower, upper, one, two))
    return (lower, *got[:2]), (upper, *got[2:])


def turn_body(bound_ref, q_ref, out_ref):
    for at in range(0, q_ref.shape[0], 256):
        out_ref[:, at : at + 256] = q_ref[at : at + 256, :].astype(F32).T.astype(BF)


def turn(bounds, query):
    out = jax.ShapeDtypeStruct(query.shape[::-1], BF)
    return call(turn_body, out, args=(bounds, query))


def three(value):
    parts = []
    for _ in range(3):
        top = value.astype(BF).astype(F32)
        parts.append(top)
        value = value - top
    return parts


def attend_body(step, begin, place_ref, qt_ref, *refs):
    count = 2 if begin else 4
    shards = [refs[3 * n : 3 * n + 3] for n in range(count)]
    if begin:
        acc_out, peak_out = refs[6:]
    else:
        acc_in, peak_in, o_ref, lse_ref, worst_ref = refs[12:]
    width = qt_ref.shape[0]
    slots = shards[0][1].shape[1]
    rows = 256
    pieces = qt_ref.shape[1] // rows
    factor = LOG2E / width**0.5
    lane = lax.broadcasted_iota(jnp.int32, (16, rows), 1)
    which = coset(row_of(place_ref) - step[0], column_of(place_ref) - step[1])

    def cuts_of(n):
        return [(n, at, 256) for at in range(0, slots, 256)] + [(n, slots, 16)] * (n % 2)

    def score(query, cut, i, exact=False):
        n, at, deep = cut
        kv_ref, vt_ref, b_ref = shards[n]
        part = jnp.dot(kv_ref[at : at + deep, :], query, preferred_element_type=F32)
        if deep == 16:
            opens = jnp.concatenate([b_ref[0:16, :]] * 2, 1)
            ends = jnp.concatenate([b_ref[16:32, :]] * 2, 1)
            member = 4 * i + (lane >> 6)
            token = 32 * member_y(which, member) + 4 * (member >> 1)
            token = token + ((lane >> 4) & 3)
            part = jnp.where((token >= opens) & (token < ends), part, -jnp.inf)
        elif exact:
            live = jnp.concatenate([b_ref[32:33, :]] * 2, 1)
            alive = lax.broadcasted_iota(jnp.int32, (deep, rows), 0) + at < live
            part = jnp.where(alive, part, -jnp.inf)
        return part

    def most(part):
        return jnp.max(part, axis=0, keepdims=True)

    def weigh(part, cut, peak, total):
        weight = jnp.exp2((part - peak) * factor).astype(BF)
        n, at, wide = cut
        if wide == 16:
            weight = jnp.concatenate([weight, jnp.zeros((112, rows), BF)], 0)
            wide = 128
        add = jnp.dot(shards[n][1][:, at : at + wide], weight, preferred_element_type=F32)
        return add if total is None else total + add

    def finish(i, peak, total):
        count = total[width : width + 1, :]
        out = total[0:width, :] * (1.0 / count)
        at = i * rows
        if not isinstance(i, int):
            at = pl.multiple_of(at, rows)
        o_ref[pl.ds(at, rows), :] = out.T.astype(BF)
        lse = peak * factor + jnp.log(count) * LOG2E
        lse_ref[i] = jnp.concatenate([lse[:, 0:128], lse[:, 128:256]], 0)
        return count

    def query_of(i):
        return qt_ref[:, i * rows : (i + 1) * rows]

    cuts = cuts_of(count - 2) + cuts_of(count - 1)
    worst = None
    todo = [(i, cut) for i in range(pieces) for cut in cuts]
    ahead = score(query_of(0), cuts[0], 0)
    peak_ahead = most(ahead)
    for at_todo, (i, cut) in enumerate(todo):
        part, at = ahead, slice(i * rows, (i + 1) * rows)
        if cut == cuts[0]:
            peak = peak_ahead if begin else peak_in[0:1, at]
            total = None if begin else acc_in[:, at]
        if at_todo + 1 < len(todo):
            j, later = todo[at_todo + 1]
            ahead = score(query_of(j), later, j)
            if begin and later == cuts[0]:
                peak_ahead = most(ahead)
        total = weigh(part, cut, peak, total)
        if cut == cuts[-1]:
            if begin:
                acc_out[:, at] = total
                peak_out[:, at] = jnp.broadcast_to(peak, (8, rows))
            else:
                counts = finish(i, peak, total)
                worst = counts if worst is None else jnp.maximum(worst, counts)
    if begin:
        return
    worst_ref[...] = jnp.broadcast_to(worst, worst_ref.shape)

    @pl.when(jnp.logical_not(jnp.max(worst_ref[0:1, :]) < HUGE))
    def _():
        def slow(i, carry):
            query = qt_ref[:, pl.ds(pl.multiple_of(i * rows, rows), rows)]
            peak, total = None, None
            every = sum((cuts_of(n) for n in range(count)), [])
            for cut in every:
                top = most(score(query, cut, i, True))
                peak = top if peak is None else jnp.maximum(peak, top)
            for cut in every:
                total = weigh(score(query, cut, i, True), cut, peak, total)
            finish(i, peak, total)
            return carry

        lax.fori_loop(0, pieces, slow, 0)

    lse = jnp.concatenate([lse_ref[i] for i in range(pieces)], 0)
    parts = three(lse) + [jnp.zeros((8, 128), F32)]
    o_ref[pieces * rows :, :] = jnp.concatenate(parts, 0).astype(BF)


def attend(place, query, near, step):
    width, rows = query.shape
    return call(
        functools.partial(attend_body, step, True),
        [
            jax.ShapeDtypeStruct((width + 16, rows), F32),
            jax.ShapeDtypeStruct((8, rows), F32),
        ],
        flops=8 * rows * near[0][1].shape[1] * 256,
        moved=8 * near[0][0].size,
        smem=1,
        args=(place, query, *near[0], *near[1]),
    )


def attend_on(place, query, near, far, sums, step):
    width, rows = query.shape
    return call(
        functools.partial(attend_body, step, False),
        jax.ShapeDtypeStruct((rows + TAIL, width), BF),
        flops=8 * rows * far[0][1].shape[1] * 256,
        moved=8 * far[0][0].size,
        scratch=[pltpu.VMEM((4, 2, 128), F32), pltpu.VMEM((8, 256), F32)],
        smem=1,
        args=(place, query, *near[0], *near[1], *far[0], *far[1], *sums),
    )


def diagonal(rows):
    return lax.broadcasted_iota(jnp.int32, (rows, 128), 0) == lax.broadcasted_iota(
        jnp.int32, (rows, 128), 1
    )


def spread(row, eye):
    return jnp.sum(jnp.where(eye, row, 0.0), axis=1, keepdims=True)


def first_body(*refs):
    ins, out_ref = refs[:-1], refs[-1]
    rows = ins[0].shape[0] - TAIL
    eye = diagonal(128)
    logs = []
    for ref in ins:
        tail = ref[rows:, :].astype(F32)
        logs.append(tail[0:8] + tail[8:16] + tail[16:24])
    top = functools.reduce(jnp.maximum, logs)
    weights = [jnp.exp2(log - top) for log in logs]
    total = functools.reduce(jnp.add, weights)
    lse = top + jnp.log(total) * LOG2E
    weights = [w / total for w in weights]
    parts = []
    for _ in range(3):
        high = lse.astype(BF).astype(F32)
        parts.append(high)
        lse = lse - high
    empty = jnp.zeros((5, 128), F32)
    for b in range(rows // 128):
        merged = None
        for ref, weight in zip(ins, weights):
            term = ref[b * 128 : (b + 1) * 128, :].astype(F32) * spread(weight[b : b + 1], eye)
            merged = term if merged is None else merged + term
        merged = merged.astype(BF)
        tail = jnp.concatenate([p[b : b + 1] for p in parts] + [empty], 0).astype(BF)
        for j in range(2):
            out_ref[2 * b + j, 0:64, :] = merged[64 * j : 64 * j + 64, :]
            out_ref[2 * b + j, 64:72, :] = tail


def first_merge(ins):
    rows, width = ins[0].shape
    out = jax.ShapeDtypeStruct(((rows - TAIL) // 64, 72, width), BF)
    return call(first_body, out, args=tuple(ins))


def second_body(place_ref, got_ref, out_ref, logs):
    parts = got_ref.shape[0]
    for c in range(parts):
        tail = got_ref[c, 64:72, :].astype(F32)
        logs[c : c + 1, :] = tail[0:1] + tail[1:2] + tail[2:3]
    lse = logs[...]
    lse = jnp.where(row_of(place_ref) >= 4, pltpu.roll(lse, 64, 1), lse)
    weight = jnp.exp2(lse - jnp.max(lse, axis=0, keepdims=True))
    weight = weight / jnp.sum(weight, axis=0, keepdims=True)
    lane = lax.broadcasted_iota(jnp.int32, (64, 128), 1)
    eye = lax.bitwise_and(lane, 63) == lax.broadcasted_iota(jnp.int32, (64, 128), 0)
    moved = pltpu.roll(weight, 64, 1)
    high, low = [], []
    for c in range(0, parts, 2):
        pair = jnp.where(lane[0:1] < 64, weight[c : c + 1], moved[c + 1 : c + 2])
        pair = jnp.where(eye, pair, 0.0)
        high.append(pair.astype(BF))
        low.append((pair - high[-1].astype(F32)).astype(BF))
    rows = jnp.concatenate([got_ref[c, 0:64, :] for c in range(parts)], 0)
    total = jnp.dot(jnp.concatenate(high, 1), rows, preferred_element_type=F32)
    total = total + jnp.dot(jnp.concatenate(low, 1), rows, preferred_element_type=F32)
    out_ref[...] = total.astype(BF)


def second_merge(place, got):
    return call(
        second_body,
        jax.ShapeDtypeStruct((64, got.shape[2]), BF),
        scratch=[pltpu.VMEM((got.shape[0], 128), F32)],
        smem=1,
        args=(place, got),
    )


def project_body(place_ref, w_ref, *refs):
    ins, out_ref, rows = refs[:4], refs[4], refs[5]
    heads = w_ref.shape[0] // ins[0].shape[1]
    tokens = rows.shape[0] // heads
    for ref, step in zip(ins, STEPS):
        which = coset(row_of(place_ref) - step[0], column_of(place_ref) - step[1])
        for n in range(ref.shape[0] // 64):
            to = pl.multiple_of(64 * (SIDE * member_y(which, n) + n // 2), 64)
            rows[pl.ds(to, 64), :] = ref[64 * n : 64 * n + 64, :].astype(F32)
    left = [rows[pl.ds(h, tokens, stride=heads), :].astype(BF) for h in range(heads)]
    mixed = jnp.dot(jnp.concatenate(left, 1), w_ref[...], preferred_element_type=F32)
    out_ref[...] = mixed.astype(BF)


def project(place, weight, ins):
    deep, cols = weight.shape
    rows, width = ins[0].shape
    tokens = 4 * rows * width // deep
    return call(
        project_body,
        jax.ShapeDtypeStruct((tokens, cols), BF),
        flops=2 * tokens * deep * cols,
        scratch=[pltpu.VMEM((4 * rows, width), F32)],
        smem=1,
        args=(place, weight, *ins),
    )


def final_body(got_ref, out_ref):
    total = got_ref[0].astype(F32)
    for i in range(1, got_ref.shape[0]):
        total = total + got_ref[i].astype(F32)
    out_ref[...] = total.astype(BF)


def local(queries, cache_keys, cache_values, new_keys, new_values, cache_len, segment, out_weight):
    place = lax.axis_index("ctx").astype(jnp.int32).reshape(1)
    block, heads, width = queries.shape
    seg = segment.reshape(-1, 128)
    near = prepare(
        cache_len,
        place,
        seg,
        cache_keys[:, 0, :],
        cache_values[:, 0, :],
        new_keys[:, 0, :],
        new_values[:, 0, :],
    )
    lower, upper = shift(near[0][0], (0, 1)), shift(near[1][0], (0, -1))
    mine = turn(near[0][2], share(queries.reshape(block * heads, width)))
    theirs = shift(mine, (1, 0))
    sums = attend(place, mine, near, (0, 0))
    their_sums = attend(place, theirs, near, (1, 0))
    far = unpack(place, seg, lower, upper, sums[1], their_sums[1])
    their_part = attend_on(place, theirs, near, far, their_sums, (1, 0))
    part = attend_on(place, mine, near, far, sums, (0, 0))
    part = first_merge([part, shift(their_part, (-1, 0))])
    own = second_merge(place, exchange(part))
    mine = share(own)
    every = [mine] + [shift(mine, step) for step in STEPS[1:]]
    mixed = project(place, out_weight, every)
    mixed = mixed.reshape(lax.axis_size("kvh"), -1, mixed.shape[1])
    got = lax.all_to_all(mixed, "kvh", 0, 0, tiled=True)
    return call(final_body, jax.ShapeDtypeStruct(got.shape[1:], BF), args=(got,))


def solution(mesh):
    in_specs = (
        P("ctx", "kvh", None),
        P("ctx", "kvh", None),
        P("ctx", "kvh", None),
        P("ctx", "kvh", None),
        P("ctx", "kvh", None),
        P("ctx"),
        P(),
        P("kvh", "ctx"),
    )
    out_specs = P("kvh", "ctx")
    return jax.shard_map(local, mesh=mesh, in_specs=in_specs, out_specs=out_specs, check_vma=False)
```

```python
import functools

import jax
import jax.numpy as jnp
from jax import lax
from jax.experimental import pallas as pl
from jax.experimental.pallas import tpu as pltpu
from jax.sharding import PartitionSpec as P

BF = jnp.bfloat16
F32 = jnp.float32
LOG2E = 1.4426950408889634
LIMIT = 48 * 1024 * 1024
HUGE = 2.0**100
SIDE = 8
STEPS = ((0, 0), (1, 0), (-1, 0), (0, 1))
TAIL = 32


def shift(value, step):
    pairs = []
    for y in range(SIDE):
        for z in range(SIDE):
            to = ((y + step[0]) % SIDE) * SIDE + (z + step[1]) % SIDE
            pairs.append((y * SIDE + z, to))
    return lax.ppermute(value, "ctx", pairs)


def row_of(place_ref):
    return lax.shift_right_logical(place_ref[0], 3)


def column_of(place_ref):
    return lax.bitwise_and(place_ref[0], SIDE - 1)


def coset(y, z):
    return lax.rem(y + 2 * z + 4 * SIDE, 4)


def member_y(which, i):
    return lax.rem(which + 2 * (i // 2), 4) + 4 * (i % 2)


def cosets():
    return [
        [((v + 2 * z) % 4 + 4 * b) * SIDE + z for z in range(SIDE) for b in range(2)]
        for v in range(4)
    ]


def exchange(value):
    return lax.all_to_all(value, "ctx", 0, 0, axis_index_groups=cosets(), tiled=True)


def copy_body(in_ref, out_ref):
    for i in range(out_ref.shape[0]):
        out_ref[i] = in_ref[...]


def share(value):
    copies = call(copy_body, jax.ShapeDtypeStruct((16,) + value.shape, BF), args=(value,))
    return exchange(copies).reshape(16 * value.shape[0], value.shape[1])


def call(body, out_shape, flops=0, moved=0, scratch=(), smem=0, args=()):
    vmem = pl.BlockSpec(memory_space=pltpu.VMEM)
    scalars = pl.BlockSpec(memory_space=pltpu.SMEM)
    specs = [scalars] * smem + [vmem] * (len(args) - smem)
    return pl.pallas_call(
        body,
        out_shape=out_shape,
        in_specs=specs,
        out_specs=jax.tree.map(lambda _: vmem, out_shape),
        scratch_shapes=list(scratch),
        compiler_params=pltpu.CompilerParams(vmem_limit_bytes=LIMIT),
        cost_estimate=pl.CostEstimate(flops=flops, bytes_accessed=moved, transcendentals=0),
    )(*args)


def turned(kv_ref, span, fresh, live, vt_ref):
    width = kv_ref.shape[1]
    slots = span - fresh
    step = 256
    for at in range(0, slots, step):
        vals = kv_ref[span + at : span + at + step, :].astype(F32)
        vt_ref[0:width, at : at + step] = vals.T.astype(BF)
        flags = lax.broadcasted_iota(jnp.int32, (16, step), 1) + at < live
        vt_ref[width:, at : at + step] = flags.astype(F32).astype(BF)
    if fresh:
        vals = kv_ref[span + slots : 2 * span, :].astype(F32)
        vals = jnp.concatenate([vals, jnp.zeros((128 - fresh, width), F32)], 0)
        vt_ref[0:width, slots:] = vals.T.astype(BF)
        flags = lax.broadcasted_iota(jnp.int32, (16, 128), 1) < 4
        vt_ref[width:, slots:] = flags.astype(F32).astype(BF)


def bounds_of(first, seg, live, b_ref):
    line = lax.broadcasted_iota(jnp.int32, (16, 128), 0)
    never = 1 << 30
    ends = jnp.full((16, 128), never, jnp.int32)
    seg = seg.astype(F32)
    spot = lax.broadcasted_iota(jnp.int32, seg.shape, 0) * 128 + lax.broadcasted_iota(
        jnp.int32, seg.shape, 1
    )

    def whole(part):
        return jnp.sum(jnp.sum(part, axis=0, keepdims=True), axis=1, keepdims=True)

    for j in range(4):
        own = whole(jnp.where(spot == first + j, seg, 0.0))
        count = whole(jnp.where(seg <= own, 1.0, 0.0))
        ends = jnp.where(line == j, count.astype(jnp.int32), ends)
    b_ref[0:16, :] = jnp.where(line < 4, line + first, never)
    b_ref[16:32, :] = ends
    b_ref[32:40, :] = jnp.zeros((8, 128), jnp.int32) + live


def prepare_body(place_ref, live_ref, seg_ref, k_ref, v_ref, fk_ref, fv_ref, *outs):
    live = live_ref[...]
    slots, width = k_ref.shape
    half = slots // 2
    step = 256
    first = k_ref[0:16, :].astype(F32)[0:1, :]
    line = lax.broadcasted_iota(jnp.int32, (16, width), 0)
    size = jnp.where(line == 0, live >> 6, jnp.where(line == 1, live & 63, 0))
    pad = jnp.zeros((16 - fk_ref.shape[0], width), F32)
    for n in range(2):
        kv_ref, vt_ref, b_ref = outs[3 * n : 3 * n + 3]
        fresh = 16 * n
        span = half + fresh
        for at in range(0, half, step):
            rows = slice(n * half + at, n * half + at + step)
            alive = lax.broadcasted_iota(jnp.int32, (step, width), 0) + n * half + at < live
            keys = jnp.where(alive, k_ref[rows, :].astype(F32), first)
            kv_ref[at : at + step, :] = keys.astype(BF)
            vals = jnp.where(alive, v_ref[rows, :].astype(F32), 0.0)
            kv_ref[span + at : span + at + step, :] = vals.astype(BF)
        if fresh:
            for at, ref in ((half, fk_ref), (span + half, fv_ref)):
                new = jnp.concatenate([ref[...].astype(F32), pad], 0)
                kv_ref[at : at + 16, :] = new.astype(BF)
        kv_ref[2 * span :, :] = size.astype(F32).astype(BF)
        turned(kv_ref, span, fresh, live - n * half, vt_ref)
        first_token = 4 * (SIDE * row_of(place_ref) + column_of(place_ref))
        if fresh:
            bounds_of(first_token, seg_ref[...], live - n * half, b_ref)
        else:
            b_ref[...] = jnp.zeros(b_ref.shape, jnp.int32) + live


def ready_shapes(half, n, width):
    return [
        jax.ShapeDtypeStruct((width + 16, half + 128 * n), BF),
        jax.ShapeDtypeStruct((40, 128), jnp.int32),
    ]


def prepare(live, place, seg, keys, vals, fresh_k, fresh_v):
    slots, width = keys.shape
    half = slots // 2
    out = []
    for n in range(2):
        out.append(jax.ShapeDtypeStruct((2 * (half + 16 * n) + 16, width), BF))
        out += ready_shapes(half, n, width)
    args = (place, live.reshape(1, 1), seg, keys, vals, fresh_k, fresh_v)
    got = call(prepare_body, out, smem=1, args=args)
    return tuple(got[:3]), tuple(got[3:])


def unpack_body(place_ref, seg_ref, lower_ref, upper_ref, one_ref, two_ref, *outs):
    for n, kv_ref in enumerate((lower_ref, upper_ref)):
        vt_ref, b_ref = outs[2 * n : 2 * n + 2]
        span = (kv_ref.shape[0] - 16) // 2
        fresh = 16 * n
        size = kv_ref[2 * span :, :].astype(F32)
        live = jnp.max(64.0 * size[0:1] + size[1:2]).astype(jnp.int32)
        live = live - n * (span - fresh)
        turned(kv_ref, span, fresh, live, vt_ref)
        from_z = lax.rem(column_of(place_ref) + 1, SIDE)
        if fresh:
            bounds_of(4 * (SIDE * row_of(place_ref) + from_z), seg_ref[...], live, b_ref)
        else:
            b_ref[...] = jnp.zeros(b_ref.shape, jnp.int32) + live


def unpack(place, seg, lower, upper, one, two):
    half, width = (lower.shape[0] - 16) // 2, lower.shape[1]
    out = ready_shapes(half, 0, width) + ready_shapes(half, 1, width)
    got = call(unpack_body, out, smem=1, args=(place, seg, lower, upper, one, two))
    return (lower, *got[:2]), (upper, *got[2:])


def turn_body(bound_ref, q_ref, out_ref):
    for at in range(0, q_ref.shape[0], 256):
        out_ref[:, at : at + 256] = q_ref[at : at + 256, :].astype(F32).T.astype(BF)


def turn(bounds, query):
    out = jax.ShapeDtypeStruct(query.shape[::-1], BF)
    return call(turn_body, out, args=(bounds, query))


def three(value):
    parts = []
    for _ in range(3):
        top = value.astype(BF).astype(F32)
        parts.append(top)
        value = value - top
    return parts


def attend_body(step, begin, place_ref, qt_ref, *refs):
    count = 2 if begin else 4
    shards = [refs[3 * n : 3 * n + 3] for n in range(count)]
    if begin:
        acc_out, peak_out = refs[6:]
    else:
        acc_in, peak_in, o_ref, lse_ref, worst_ref = refs[12:]
    width = qt_ref.shape[0]
    slots = shards[0][1].shape[1]
    rows = 256
    heads = 16
    pieces = qt_ref.shape[1] // rows
    factor = LOG2E / width**0.5
    lane = lax.broadcasted_iota(jnp.int32, (16, rows), 1)
    which = coset(row_of(place_ref) - step[0], column_of(place_ref) - step[1])

    def cuts_of(n):
        return [(n, at, 256) for at in range(0, slots, 256)] + [(n, slots, 16)] * (n % 2)

    def score(query, cut, i, exact=False):
        n, at, deep = cut
        kv_ref, vt_ref, b_ref = shards[n]
        part = jnp.dot(kv_ref[at : at + deep, :], query, preferred_element_type=F32)
        if deep == 16:
            opens = jnp.concatenate([b_ref[0:16, :]] * 2, 1)
            ends = jnp.concatenate([b_ref[16:32, :]] * 2, 1)
            member = 4 * i + lane // 64
            token = 32 * member_y(which, member) + 4 * (member // 2)
            token = token + lax.rem(lane // heads, 4)
            part = jnp.where((token >= opens) & (token < ends), part, -jnp.inf)
        elif exact:
            live = jnp.concatenate([b_ref[32:33, :]] * 2, 1)
            alive = lax.broadcasted_iota(jnp.int32, (deep, rows), 0) + at < live
            part = jnp.where(alive, part, -jnp.inf)
        return part

    def most(part):
        return jnp.max(part, axis=0, keepdims=True)

    def weigh(part, cut, peak, total):
        weight = jnp.exp2((part - peak) * factor).astype(BF)
        n, at, wide = cut
        if wide == 16:
            weight = jnp.concatenate([weight, jnp.zeros((112, rows), BF)], 0)
            wide = 128
        add = jnp.dot(shards[n][1][:, at : at + wide], weight, preferred_element_type=F32)
        return add if total is None else total + add

    def finish(i, peak, total):
        count = total[width : width + 1, :]
        out = total[0:width, :] * (1.0 / count)
        at = i * rows
        if not isinstance(i, int):
            at = pl.multiple_of(at, rows)
        o_ref[pl.ds(at, rows), :] = out.T.astype(BF)
        lse = peak * factor + jnp.log(count) * LOG2E
        lse_ref[i] = jnp.concatenate([lse[:, 0:128], lse[:, 128:256]], 0)
        return count

    def query_of(i):
        return qt_ref[:, i * rows : (i + 1) * rows]

    cuts = cuts_of(count - 2) + cuts_of(count - 1)
    worst = None
    todo = [(i, cut) for i in range(pieces) for cut in cuts]
    ahead = score(query_of(0), cuts[0], 0)
    peak_ahead = most(ahead)
    for at_todo, (i, cut) in enumerate(todo):
        part, at = ahead, slice(i * rows, (i + 1) * rows)
        if cut == cuts[0]:
            peak = peak_ahead if begin else peak_in[0:1, at]
            total = None if begin else acc_in[:, at]
        if at_todo + 1 < len(todo):
            j, later = todo[at_todo + 1]
            ahead = score(query_of(j), later, j)
            if begin and later == cuts[0]:
                peak_ahead = most(ahead)
        total = weigh(part, cut, peak, total)
        if cut == cuts[-1]:
            if begin:
                acc_out[:, at] = total
                peak_out[:, at] = jnp.broadcast_to(peak, (8, rows))
            else:
                counts = finish(i, peak, total)
                worst = counts if worst is None else jnp.maximum(worst, counts)
    if begin:
        return
    worst_ref[...] = jnp.broadcast_to(worst, worst_ref.shape)

    @pl.when(jnp.logical_not(jnp.max(worst_ref[0:1, :]) < HUGE))
    def _():
        def slow(i, carry):
            query = qt_ref[:, pl.ds(pl.multiple_of(i * rows, rows), rows)]
            peak, total = None, None
            every = sum((cuts_of(n) for n in range(count)), [])
            for cut in every:
                top = most(score(query, cut, i, True))
                peak = top if peak is None else jnp.maximum(peak, top)
            for cut in every:
                total = weigh(score(query, cut, i, True), cut, peak, total)
            finish(i, peak, total)
            return carry

        lax.fori_loop(0, pieces, slow, 0)

    lse = jnp.concatenate([lse_ref[i] for i in range(pieces)], 0)
    parts = three(lse) + [jnp.zeros((8, 128), F32)]
    o_ref[pieces * rows :, :] = jnp.concatenate(parts, 0).astype(BF)


def attend(place, query, near, step):
    width, rows = query.shape
    return call(
        functools.partial(attend_body, step, True),
        [
            jax.ShapeDtypeStruct((width + 16, rows), F32),
            jax.ShapeDtypeStruct((8, rows), F32),
        ],
        flops=8 * rows * near[0][1].shape[1] * 256,
        moved=8 * near[0][0].size,
        smem=1,
        args=(place, query, *near[0], *near[1]),
    )


def attend_on(place, query, near, far, sums, step):
    width, rows = query.shape
    return call(
        functools.partial(attend_body, step, False),
        jax.ShapeDtypeStruct((rows + TAIL, width), BF),
        flops=8 * rows * far[0][1].shape[1] * 256,
        moved=8 * far[0][0].size,
        scratch=[pltpu.VMEM((4, 2, 128), F32), pltpu.VMEM((8, 256), F32)],
        smem=1,
        args=(place, query, *near[0], *near[1], *far[0], *far[1], *sums),
    )


def diagonal(rows):
    return lax.broadcasted_iota(jnp.int32, (rows, 128), 0) == lax.broadcasted_iota(
        jnp.int32, (rows, 128), 1
    )


def spread(row, eye):
    return jnp.sum(jnp.where(eye, row, 0.0), axis=1, keepdims=True)


def first_body(*refs):
    ins, out_ref = refs[:-1], refs[-1]
    rows = ins[0].shape[0] - TAIL
    eye = diagonal(128)
    logs = []
    for ref in ins:
        tail = ref[rows:, :].astype(F32)
        logs.append(tail[0:8] + tail[8:16] + tail[16:24])
    top = functools.reduce(jnp.maximum, logs)
    weights = [jnp.exp2(log - top) for log in logs]
    total = functools.reduce(jnp.add, weights)
    lse = top + jnp.log(total) * LOG2E
    weights = [w / total for w in weights]
    parts = []
    for _ in range(3):
        high = lse.astype(BF).astype(F32)
        parts.append(high)
        lse = lse - high
    empty = jnp.zeros((5, 128), F32)
    for b in range(rows // 128):
        merged = None
        for ref, weight in zip(ins, weights):
            term = ref[b * 128 : (b + 1) * 128, :].astype(F32) * spread(weight[b : b + 1], eye)
            merged = term if merged is None else merged + term
        merged = merged.astype(BF)
        tail = jnp.concatenate([p[b : b + 1] for p in parts] + [empty], 0).astype(BF)
        for j in range(2):
            out_ref[2 * b + j, 0:64, :] = merged[64 * j : 64 * j + 64, :]
            out_ref[2 * b + j, 64:72, :] = tail


def first_merge(ins):
    rows, width = ins[0].shape
    out = jax.ShapeDtypeStruct(((rows - TAIL) // 64, 72, width), BF)
    return call(first_body, out, args=tuple(ins))


def second_body(place_ref, got_ref, out_ref, logs):
    parts = got_ref.shape[0]
    for c in range(parts):
        tail = got_ref[c, 64:72, :].astype(F32)
        logs[c : c + 1, :] = tail[0:1] + tail[1:2] + tail[2:3]
    lse = logs[...]
    lse = jnp.where(row_of(place_ref) // 4 == 1, pltpu.roll(lse, 64, 1), lse)
    weight = jnp.exp2(lse - jnp.max(lse, axis=0, keepdims=True))
    weight = weight / jnp.sum(weight, axis=0, keepdims=True)
    lane = lax.broadcasted_iota(jnp.int32, (64, 128), 1)
    eye = lax.bitwise_and(lane, 63) == lax.broadcasted_iota(jnp.int32, (64, 128), 0)
    moved = pltpu.roll(weight, 64, 1)
    high, low = [], []
    for c in range(0, parts, 2):
        pair = jnp.where(lane[0:1] < 64, weight[c : c + 1], moved[c + 1 : c + 2])
        pair = jnp.where(eye, pair, 0.0)
        high.append(pair.astype(BF))
        low.append((pair - high[-1].astype(F32)).astype(BF))
    rows = jnp.concatenate([got_ref[c, 0:64, :] for c in range(parts)], 0)
    total = jnp.dot(jnp.concatenate(high, 1), rows, preferred_element_type=F32)
    total = total + jnp.dot(jnp.concatenate(low, 1), rows, preferred_element_type=F32)
    out_ref[...] = total.astype(BF)


def second_merge(place, got):
    return call(
        second_body,
        jax.ShapeDtypeStruct((64, got.shape[2]), BF),
        scratch=[pltpu.VMEM((got.shape[0], 128), F32)],
        smem=1,
        args=(place, got),
    )


def project_body(place_ref, w_ref, *refs):
    ins, out_ref, rows = refs[:4], refs[4], refs[5]
    heads = w_ref.shape[0] // ins[0].shape[1]
    tokens = rows.shape[0] // heads
    for ref, step in zip(ins, STEPS):
        which = coset(row_of(place_ref) - step[0], column_of(place_ref) - step[1])
        for n in range(ref.shape[0] // 64):
            to = pl.multiple_of(64 * (SIDE * member_y(which, n) + n // 2), 64)
            rows[pl.ds(to, 64), :] = ref[64 * n : 64 * n + 64, :].astype(F32)
    left = [rows[pl.ds(h, tokens, stride=heads), :].astype(BF) for h in range(heads)]
    mixed = jnp.dot(jnp.concatenate(left, 1), w_ref[...], preferred_element_type=F32)
    out_ref[...] = mixed.astype(BF)


def project(place, weight, ins):
    deep, cols = weight.shape
    rows, width = ins[0].shape
    tokens = 4 * rows * width // deep
    return call(
        project_body,
        jax.ShapeDtypeStruct((tokens, cols), BF),
        flops=2 * tokens * deep * cols,
        scratch=[pltpu.VMEM((4 * rows, width), F32)],
        smem=1,
        args=(place, weight, *ins),
    )


def final_body(got_ref, out_ref):
    total = got_ref[0].astype(F32)
    for i in range(1, got_ref.shape[0]):
        total = total + got_ref[i].astype(F32)
    out_ref[...] = total.astype(BF)


def local(queries, cache_keys, cache_values, new_keys, new_values, cache_len, segment, out_weight):
    place = lax.axis_index("ctx").astype(jnp.int32).reshape(1)
    block, heads, width = queries.shape
    seg = segment.reshape(-1, 128)
    near = prepare(
        cache_len,
        place,
        seg,
        cache_keys[:, 0, :],
        cache_values[:, 0, :],
        new_keys[:, 0, :],
        new_values[:, 0, :],
    )
    lower, upper = shift(near[0][0], (0, 1)), shift(near[1][0], (0, -1))
    mine = turn(near[0][2], share(queries.reshape(block * heads, width)))
    theirs = shift(mine, (1, 0))
    sums = attend(place, mine, near, (0, 0))
    their_sums = attend(place, theirs, near, (1, 0))
    far = unpack(place, seg, lower, upper, sums[1], their_sums[1])
    their_part = attend_on(place, theirs, near, far, their_sums, (1, 0))
    part = attend_on(place, mine, near, far, sums, (0, 0))
    part = first_merge([part, shift(their_part, (-1, 0))])
    own = second_merge(place, exchange(part))
    mine = share(own)
    every = [mine] + [shift(mine, step) for step in STEPS[1:]]
    mixed = project(place, out_weight, every)
    mixed = mixed.reshape(lax.axis_size("kvh"), -1, mixed.shape[1])
    got = lax.all_to_all(mixed, "kvh", 0, 0, tiled=True)
    return call(final_body, jax.ShapeDtypeStruct(got.shape[1:], BF), args=(got,))


def solution(mesh):
    in_specs = (
        P("ctx", "kvh", None),
        P("ctx", "kvh", None),
        P("ctx", "kvh", None),
        P("ctx", "kvh", None),
        P("ctx", "kvh", None),
        P("ctx"),
        P(),
        P("kvh", "ctx"),
    )
    out_specs = P("kvh", "ctx")
    return jax.shard_map(local, mesh=mesh, in_specs=in_specs, out_specs=out_specs, check_vma=False)
```
